512 devices in a mesh: row: 16 (over y, x_hi, core), col: 32 (over z, x_lo).
Axes of the slice: x: 4 (x_hi: 2, x_lo: 2; x = x_hi * 2 + x_lo), y: 4, z: 16, core: 2. Of those that a mesh axis runs over, the one named last changes fastest.
Arguments:
- ancestor_inverse: float32 [4096, 4096], P('row', 'col'), may hold values from -6 to 6
- pattern: int32 [32, 32], replicated, may hold values 0 or 1
- listed: int32 [2, 16], replicated, may hold values from 0 to 31, as said below
- panels: float32 [2, 4096, 512], P(None, ('col', 'row')), may hold values from -0.09375 to 0.09375
- parent_panels: float32 [1, 512, 512], replicated, may hold values from -0.25 to 0.25
- diag_inverse: float32 [2, 512, 512], P(None, 'row', 'col'), may hold values from -6 to 6
Outputs:
- upper_blocks: float32 [2, 4096, 512], P(None, ('col', 'row'))
- diagonal_blocks: float32 [2, 512, 512], P(None, 'row', 'col')
The draws below stay inside these ranges and needn't reach their ends.
Inputs may be any that keep to these rules, and one draw needn't show every extreme that they name: Each row of listed names 16 different blocks.
All inputs are finite; a program needn't handle non-finite values.
Results may differ from the reference program's by a relative error of at most 0.00011.
Values sent between devices are 32-bit elements; how exact they have to be, the bound alone decides.
A program may use at most 64 MiB of HBM per device.

```python
import jax
import jax.numpy as jnp
from jax import lax

W = 512
BLK = 128
SUPER = 2
NANC = 4096
LISTED = 16


def draw_listed(key, part):
    chosen = []
    for supernode in range(SUPER):
        order = jax.random.permutation(jax.random.fold_in(key, 17 + supernode), NANC // BLK)
        chosen.append(order[:LISTED])
    return jnp.stack(chosen).astype(jnp.int32)


def set_ends(entries, stream_key, least, top_value):
    shape = entries.shape
    spot = [jax.random.randint(jax.random.fold_in(stream_key, axis), (), 0, shape[axis]) for axis in range(len(shape))]
    entries = entries.at[tuple(spot)].set(least)
    longest = shape.index(max(shape))
    spot[longest] = (spot[longest] + 1) % shape[longest]
    return entries.at[tuple(spot)].set(top_value)


def shard_levels(own_key, extent, cuts, low, top_value):
    def one(dim, shards_of):
        steps = jax.random.uniform(jax.random.fold_in(jax.random.fold_in(own_key, 6), dim), (shards_of,), jnp.float32, low / len(cuts), top_value / len(cuts))
        return jnp.repeat(jnp.exp(steps), extent[dim] // shards_of).reshape((-1,) + (1,) * (len(extent) - dim - 1))

    loudness = one(*cuts[0])
    for cut in cuts[1:]:
        loudness = loudness * one(*cut)
    return loudness


def gaussian(stream_key, extent, spread, reach, cuts=(), held_as=jnp.bfloat16):
    values = jax.random.normal(stream_key, extent, jnp.float32) * spread
    if len(cuts) > 0:
        values = shard_levels(stream_key, extent, cuts, -0.22, 0.18) * values
    return jnp.clip(values, min=-reach, max=reach).astype(held_as)


def setup_inputs(seed: int = 0) -> dict:
    keys = jax.random.split(jax.random.key(seed), 7)
    ancestor_inverse = gaussian(keys[0], (NANC, NANC), 1.0, 6.0, ((0, 16), (1, 32)), jnp.float32)
    pattern = set_ends((jax.random.randint(keys[1], (NANC // BLK, NANC // BLK), 0, 4) < 3).astype(jnp.int32), jax.random.fold_in(keys[1], 1), 0, 1)
    listed = draw_listed(jax.random.fold_in(keys[6], 71), 0)
    panels = gaussian(keys[3], (SUPER, NANC, W), NANC ** -0.5, 0.09375, ((1, 512),), jnp.float32)
    parent_panels = gaussian(keys[4], (SUPER - 1, W, W), W ** -0.5, 0.25, (), jnp.float32)
    diag_inverse = gaussian(keys[5], (SUPER, W, W), 1.0, 6.0, ((1, 16), (2, 32)), jnp.float32)
    return dict(ancestor_inverse=ancestor_inverse, pattern=pattern, listed=listed, panels=panels, parent_panels=parent_panels, diag_inverse=diag_inverse)


def contract_rows(left, right):
    return lax.dot_general(left, right, (((0,), (0,)), ((), ())), precision=lax.Precision.HIGHEST, preferred_element_type=jnp.float32)


def reference(ancestor_inverse, pattern, listed, panels, parent_panels, diag_inverse):
    highest = lax.Precision.HIGHEST
    blocks = NANC // BLK
    masked = (ancestor_inverse.reshape(blocks, BLK, blocks, BLK) * pattern.astype(jnp.float32)[:, None, :, None]).reshape(NANC, NANC)
    block_ids = jnp.arange(blocks, dtype=jnp.int32)
    listed_flags = jnp.any(listed[:, :, None] == block_ids[None, None, :], axis=1).astype(jnp.float32)
    row_keep = jnp.repeat(listed_flags, BLK, axis=1)
    uppers = []
    diagonals = []
    for supernode in range(SUPER):
        kept_panel = panels[supernode] * row_keep[supernode][:, None]
        column_sum = contract_rows(masked, kept_panel)
        if supernode > 0:
            parent_link = parent_panels[supernode - 1]
            chained = jnp.dot(uppers[-1], parent_link, precision=highest, preferred_element_type=jnp.float32)
            column_sum = column_sum + chained
        upper_part = -column_sum * row_keep[supernode][:, None]
        diagonal = diag_inverse[supernode] - contract_rows(kept_panel, upper_part)
        if supernode > 0:
            carried = jnp.dot(diagonals[-1], parent_link, precision=highest, preferred_element_type=jnp.float32)
            diagonal = diagonal + contract_rows(chained, kept_panel) + contract_rows(parent_link, carried)
        uppers.append(upper_part)
        diagonals.append(diagonal)
    return jnp.stack(uppers), jnp.stack(diagonals)
```

```python
import functools

import jax
import jax.numpy as jnp
from jax import lax
from jax.experimental import pallas as pl
from jax.experimental.pallas import tpu as pltpu
from jax.sharding import PartitionSpec as P

BLK = 128
LANES = 128
MESH = pl.DeviceIdType.MESH
F32 = jnp.float32


def dot(left, right):
    return jnp.dot(left, right, precision=lax.Precision.HIGHEST, preferred_element_type=F32)


def dot_rows(left, right):
    return lax.dot_general(
        left,
        right,
        (((0,), (0,)), ((), ())),
        precision=lax.Precision.HIGHEST,
        preferred_element_type=F32,
    )


def exchange(parts, width):
    parts = list(parts)
    count = len(parts)
    segment = lax.broadcasted_iota(jnp.int32, parts[0].shape, 1) // width
    bit = count // 2
    while bit:
        low = (segment % (2 * bit)) < bit
        for a in range(count):
            if a & bit == 0:
                first, second = parts[a], parts[a + bit]
                parts[a] = jnp.where(low, first, pltpu.roll(second, bit * width, 1))
                parts[a + bit] = jnp.where(low, pltpu.roll(first, LANES - bit * width, 1), second)
        bit //= 2
    return parts


def kernel(
    rows,
    cols,
    a_ref,
    pattern_ref,
    listed_ref,
    panel_ref,
    link_ref,
    diag_ref,
    upper_ref,
    out_ref,
    panels,
    anc,
    slab,
    partial,
    shares,
    left_out,
    left_in,
    kept_out,
    kept_in,
    upper_in,
    sum_out,
    sum_in,
    band,
    tile_out,
    tile_in,
    anc_send,
    anc_recv,
    ring_send,
    ring_recv,
    sems,
):
    row, col = lax.axis_index("row"), lax.axis_index("col")
    depth = cols // 2
    z, side = lax.div(col, 2), lax.rem(col, 2)
    pair, core = lax.div(row, 2), lax.rem(row, 2)
    height = panel_ref.shape[1]
    width = panel_ref.shape[2]
    half = width // 2
    plane = 2 * rows
    me = side * rows + row
    tall = a_ref.shape[0]
    band_rows = width // rows
    band_cols = width // cols

    def place(index):
        return (lax.rem(index, rows), 2 * z + lax.div(index, rows))

    def peer(step):
        return lax.rem(me + step, plane)

    with jax.named_scope("greet"):
        barrier = pltpu.get_barrier_semaphore()

        @pl.loop(1, plane)
        def _(step):
            pl.semaphore_signal(barrier, inc=1, device_id=place(peer(step)), device_id_type=MESH)

        @pl.loop(2, cols)
        def _(step):
            other = lax.rem(2 * z + step, cols)
            pl.semaphore_signal(barrier, inc=1, device_id=(row, other), device_id_type=MESH)

        def keep(s):
            found = listed_ref[s, 0] == col
            for i in range(1, listed_ref.shape[1]):
                found = jnp.logical_or(found, listed_ref[s, i] == col)
            return jnp.where(found, 1.0, 0.0).astype(F32)

        flag0, flag1 = keep(0), keep(1)
        kept0 = panel_ref[0] * flag0
        kept1 = panel_ref[1] * flag1
        panels[z, 0] = kept0
        panels[z, 1] = kept1
        for i in range(tall // BLK):
            present = pattern_ref[(tall // BLK) * row + i, col].astype(F32)
            anc[side, pl.ds(core * tall + i * BLK, BLK), :] = a_ref[pl.ds(i * BLK, BLK), :] * present
        pl.semaphore_wait(barrier, plane - 1 + cols - 2)

    def ring(step, right, part=slice(None)):
        sign = -1 if right else 1
        block = lax.rem(z + depth + sign * step, depth)
        target = lax.rem(col + (2 if right else cols - 2), cols)
        piece = panels.at[block] if isinstance(part, slice) else panels.at[block, part]
        way = 0 if right else 1
        return pltpu.make_async_remote_copy(
            src_ref=piece,
            dst_ref=piece,
            send_sem=ring_send.at[way, step],
            recv_sem=ring_recv.at[way, step],
            device_id=(row, target),
            device_id_type=MESH,
        )

    slab_sent, slab_got, left_sent, left_got, kept_sent, kept_got = (sems.at[i] for i in range(6))
    share_sent, share_got, upper_sent, upper_got, sum_sent, sum_got = (sems.at[i] for i in range(6, 12))
    tile_sent, tile_got = sems.at[12], sems.at[13]

    def spread(offset):
        block = lax.rem(z + depth + offset, depth)
        owner = lax.div(block, 2)
        slot = (lax.rem(block, 2) * 2 + side) * rows + row
        for step in range(4):
            quarter = lax.rem(2 * core + side + step, 4)
            super_of, half_of = lax.div(quarter, 2), lax.rem(quarter, 2)
            source = panels.at[block, super_of, :, pl.ds(pl.multiple_of(half_of * half, LANES), half)]

            def send():
                pltpu.make_async_remote_copy(
                    src_ref=source,
                    dst_ref=slab.at[slot],
                    send_sem=slab_sent,
                    recv_sem=slab_got,
                    device_id=(2 * owner + super_of, 2 * z + half_of),
                    device_id_type=MESH,
                ).start()

            if step == 0:
                pl.when(owner != pair)(send)

                @pl.when(owner == pair)
                def _():
                    pltpu.make_async_copy(source, slab.at[slot], slab_got).start()
            else:
                send()

    def anc_copy(i):
        other_row = 2 * pair + (core + i) % 2
        other_col = 2 * z + (side + i // 2) % 2
        piece = anc.at[side, pl.ds(core * tall, tall), :]
        return pltpu.make_async_remote_copy(
            src_ref=piece,
            dst_ref=piece,
            send_sem=anc_send.at[i - 1],
            recv_sem=anc_recv.at[i - 1],
            device_id=(other_row, other_col),
            device_id_type=MESH,
        )

    steps = depth // 2
    with jax.named_scope("start"):
        ring(0, True).start()
        ring(0, False).start()
        for i in (1, 2, 3):
            anc_copy(i).start()
        spread(0)

    with jax.named_scope("early"):
        chained_kept = dot(kept0, link_ref[...])
        mixed = kept1 - chained_kept
        tile = diag_ref[0]
        link_band = link_ref[pl.ds(pl.multiple_of(row * band_rows, 8), band_rows), :]
        extra = dot_rows(tile, link_band)
        per = LANES // band_rows
        for g in range(width // LANES):
            cut = slice(g * LANES, (g + 1) * LANES)
            packed = exchange([kept0[:, cut], kept1[:, cut], mixed[:, cut], extra[:height, cut]], band_rows)
            for j in range(per):
                left_out[g * per + j, :, :LANES] = packed[j]
                tail = extra[height:, cut]
                if j:
                    tail = pltpu.roll(tail, LANES - j * band_rows, 1)
                left_out[g * per + j, :, LANES:] = tail
        for h in range(2):
            kept_out[h] = kept1[:, h * half : (h + 1) * half]
        left_in[me] = left_out[row]
        kept_in[me] = kept_out[side]

        @pl.loop(1, plane)
        def _(step):
            other = peer(step)
            target = place(other)
            pltpu.make_async_remote_copy(
                src_ref=left_out.at[target[0]],
                dst_ref=left_in.at[me],
                send_sem=left_sent,
                recv_sem=left_got,
                device_id=target,
                device_id_type=MESH,
            ).start()
            pltpu.make_async_remote_copy(
                src_ref=kept_out.at[lax.div(other, rows)],
                dst_ref=kept_in.at[me],
                send_sem=kept_sent,
                recv_sem=kept_got,
                device_id=target,
                device_id_type=MESH,
            ).start()

    with jax.named_scope("ring"):

        @pl.loop(0, steps - 1)
        def _(step):
            ring(step, True).wait_recv()
            ring(step, False).wait_recv()

            @pl.when(step < steps - 2)
            def _():
                ring(step + 1, True).start()
                ring(step + 1, False).start()

            @pl.when(step == steps - 2)
            def _():
                ring(steps - 1, True, 0).start()
                ring(steps - 1, False, 1).start()

            spread(-step - 1)
            spread(step + 1)

        ring(steps - 1, True, 0).wait_recv()
        ring(steps - 1, False, 1).wait_recv()
        spread(steps)

    def wait_for(ref, sem):
        pltpu.make_async_copy(ref, ref, sem).wait()

    with jax.named_scope("slab"):
        for i in (1, 2, 3):
            anc_copy(i).wait_recv()
        wait_for(slab, slab_got)
    with jax.named_scope("product"):
        kept_rows = slab[...].reshape(2 * tall, half)
        for i in range(2):
            part = dot_rows(anc[i], kept_rows)
            partial[pl.ds(i * rows, rows)] = part.reshape(rows, height, half)

    slot = (2 * core + side) * (rows // 2) + pair
    with jax.named_scope("scatter"):
        shares[slot] = partial[me]

        @pl.loop(1, plane)
        def _(step):
            other = peer(step)
            pltpu.make_async_remote_copy(
                src_ref=partial.at[other],
                dst_ref=shares.at[slot],
                send_sem=share_sent,
                recv_sem=share_got,
                device_id=place(other),
                device_id_type=MESH,
            ).start()

    with jax.named_scope("linkterm"):
        wait_for(left_in.at[pl.ds(0, plane - 1)], left_got)
        wait_for(kept_in.at[pl.ds(0, plane - 1)], kept_got)
        lefts = left_in[...].reshape(plane * height, 2 * LANES)
        kept_half = kept_in[...].reshape(plane * height, half)
        column_half = pl.ds(pl.multiple_of(side * half, LANES), half)
        link_half = link_ref[:, column_half]
        group = pl.ds(pl.multiple_of(lax.div(row, per) * LANES, LANES), LANES)
        link_group = link_ref[:, group]
        link_rows = link_ref[pl.ds(pl.multiple_of(z * 2 * band_cols, 8), 2 * band_cols), column_half]

        def repeat(i):
            return jnp.concatenate(
                [link_rows[s * band_cols + i : s * band_cols + i + height] for s in range(2) for _ in range(rows)],
                axis=0,
            )

        constant = (
            dot_rows(lefts[:, :LANES], repeat(0))[3 * band_rows :]
            + dot_rows(lefts[:, LANES:], repeat(height))[:band_rows]
        )

    with jax.named_scope("shares"):
        wait_for(shares.at[pl.ds(0, plane - 1)], share_got)
        quarters = []
        for q in range(4):
            total = shares[q * (rows // 2)]
            for i in range(1, rows // 2):
                total = total + shares[q * (rows // 2) + i]
            quarters.append(total)
        sum0 = jnp.concatenate(quarters[:2], axis=1)
        sum1 = jnp.concatenate(quarters[2:], axis=1)
        upper0 = -sum0 * flag0
        upper_in[me] = upper0
        sum_out[0] = quarters[2]
        sum_out[1] = quarters[3]
        sum_in[me] = sum_out[side]

    with jax.named_scope("gather"):

        @pl.loop(1, plane)
        def _(step):
            other = peer(step)
            target = place(other)
            pltpu.make_async_remote_copy(
                src_ref=upper_in.at[me],
                dst_ref=upper_in.at[me],
                send_sem=upper_sent,
                recv_sem=upper_got,
                device_id=target,
                device_id_type=MESH,
            ).start()
            pltpu.make_async_remote_copy(
                src_ref=sum_out.at[lax.div(other, rows)],
                dst_ref=sum_in.at[me],
                send_sem=sum_sent,
                recv_sem=sum_got,
                device_id=target,
                device_id_type=MESH,
            ).start()

        upper_ref[0] = upper0
        upper_ref[1] = -(sum1 + dot(upper0, link_ref[...])) * flag1
        wait_for(upper_in.at[pl.ds(0, plane - 1)], upper_got)
        wait_for(sum_in.at[pl.ds(0, plane - 1)], sum_got)

    with jax.named_scope("diagonal"):
        uppers = upper_in[...].reshape(plane * height, width)
        sums = sum_in[...].reshape(plane * height, half)
        chained_half = dot(uppers, link_half)
        chained_group = dot(uppers, link_group)
        band[...] = dot_rows(chained_group, kept_half)
        crossed = band[pl.ds(pl.multiple_of(lax.rem(row, per) * band_rows, 8), band_rows), :]
        upper_half = upper_in[:, :, column_half].reshape(plane * height, half)
        first = lefts[:, :LANES]
        tile0 = -dot_rows(first, upper_half)[:band_rows]
        tile1 = (
            dot_rows(first, sums)[band_rows : 2 * band_rows]
            + dot_rows(first, chained_half)[2 * band_rows : 3 * band_rows]
            + crossed
            + constant
        )
        share = LANES // band_cols
        for g in range(half // LANES):
            cut = slice(g * LANES, (g + 1) * LANES)
            pieces = [t[8 * i : 8 * i + 8, cut] for t in (tile0, tile1) for i in range(band_rows // 8)]
            for j, packed in enumerate(exchange(pieces, band_cols)):
                tile_out[g * share + j] = packed

    count = cols // 2
    own = lax.div(col, count) == side
    with jax.named_scope("tiles"):

        @pl.loop(0, count)
        def _(step):
            other = lax.rem(col + step, count)
            target = side * count + other

            @pl.when(target != col)
            def _():
                pltpu.make_async_remote_copy(
                    src_ref=tile_out.at[other],
                    dst_ref=tile_in.at[z],
                    send_sem=tile_sent,
                    recv_sem=tile_got,
                    device_id=(row, target),
                    device_id_type=MESH,
                ).start()

            @pl.when(target == col)
            def _():
                pltpu.make_async_copy(tile_out.at[other], tile_in.at[z], tile_got).start()

        wait_for(tile_in, tile_got)
        total = tile_in[0]
        for i in range(1, count):
            total = total + tile_in[i]
        for s in range(2):
            for i in range(band_rows // 8):
                at = (s * (band_rows // 8) + i) * band_cols
                out_ref[s, 8 * i : 8 * i + 8, :] = (
                    diag_ref[s, 8 * i : 8 * i + 8, :] + total[:, at : at + band_cols]
                )

    with jax.named_scope("drain"):
        for i in (1, 2, 3):
            anc_copy(i).wait_send()

        @pl.loop(0, steps - 1)
        def _(step):
            ring(step, True).wait_send()
            ring(step, False).wait_send()

        ring(steps - 1, True, 0).wait_send()
        ring(steps - 1, False, 1).wait_send()
        wait_for(slab.at[pl.ds(0, 4 * rows - 2)], slab_sent)
        wait_for(left_in.at[pl.ds(0, plane - 1)], left_sent)
        wait_for(kept_in.at[pl.ds(0, plane - 1)], kept_sent)
        wait_for(shares.at[pl.ds(0, plane - 1)], share_sent)
        wait_for(upper_in.at[pl.ds(0, plane - 1)], upper_sent)
        wait_for(sum_in.at[pl.ds(0, plane - 1)], sum_sent)

        @pl.when(own)
        def _():
            wait_for(tile_in.at[pl.ds(0, count - 1)], tile_sent)

        @pl.when(jnp.logical_not(own))
        def _():
            wait_for(tile_in, tile_sent)


def local(rows, cols, ancestor_inverse, pattern, listed, panels, parent_panels, diag_inverse):
    supers, height, width = panels.shape
    tall, wide = ancestor_inverse.shape
    depth = cols // 2
    plane = 2 * rows
    half = width // 2
    count = cols // 2
    vmem = pl.BlockSpec(memory_space=pltpu.VMEM)
    smem = pl.BlockSpec(memory_space=pltpu.SMEM)
    return pl.pallas_call(
        functools.partial(kernel, rows, cols),
        out_shape=(
            jax.ShapeDtypeStruct(panels.shape, F32),
            jax.ShapeDtypeStruct(diag_inverse.shape, F32),
        ),
        in_specs=[vmem, smem, smem, vmem, vmem, vmem],
        out_specs=(vmem, vmem),
        scratch_shapes=[
            pltpu.VMEM((depth, supers, height, width), F32),
            pltpu.VMEM((2, 2 * tall, wide), F32),
            pltpu.VMEM((4 * rows, height, half), F32),
            pltpu.VMEM((plane, height, half), F32),
            pltpu.VMEM((plane, height, half), F32),
            pltpu.VMEM((rows, height, 2 * LANES), F32),
            pltpu.VMEM((plane, height, 2 * LANES), F32),
            pltpu.VMEM((2, height, half), F32),
            pltpu.VMEM((plane, height, half), F32),
            pltpu.VMEM((plane, height, width), F32),
            pltpu.VMEM((2, height, half), F32),
            pltpu.VMEM((plane, height, half), F32),
            pltpu.VMEM((LANES, half), F32),
            pltpu.VMEM((count, 8, LANES), F32),
            pltpu.VMEM((count, 8, LANES), F32),
            pltpu.SemaphoreType.DMA((3,)),
            pltpu.SemaphoreType.DMA((3,)),
            pltpu.SemaphoreType.DMA((2, depth // 2)),
            pltpu.SemaphoreType.DMA((2, depth // 2)),
            pltpu.SemaphoreType.DMA((14,)),
        ],
        compiler_params=pltpu.CompilerParams(
            collective_id=0, has_side_effects=True, vmem_limit_bytes=48 * 1024 * 1024
        ),
    )(ancestor_inverse, pattern, listed, panels, parent_panels[0], diag_inverse)


def solution(mesh):
    rows, cols = mesh.shape["row"], mesh.shape["col"]
    return jax.shard_map(
        functools.partial(local, rows, cols),
        mesh=mesh,
        in_specs=(
            P("row", "col"),
            P(),
            P(),
            P(None, ("col", "row"), None),
            P(),
            P(None, "row", "col"),
        ),
        out_specs=(P(None, ("col", "row"), None), P(None, "row", "col")),
        check_vma=False,
    )
```

```python
import functools

import jax
import jax.numpy as jnp
from jax import lax
from jax.experimental import pallas as pl
from jax.experimental.pallas import tpu as pltpu
from jax.sharding import PartitionSpec as P

BLK = 128
LANES = 128
MESH = pl.DeviceIdType.MESH
F32 = jnp.float32


def dot(left, right):
    return jnp.dot(left, right, precision=lax.Precision.HIGHEST, preferred_element_type=F32)


def dot_rows(left, right):
    return lax.dot_general(
        left,
        right,
        (((0,), (0,)), ((), ())),
        precision=lax.Precision.HIGHEST,
        preferred_element_type=F32,
    )


def exchange(parts, width):
    parts = list(parts)
    count = len(parts)
    segment = lax.broadcasted_iota(jnp.int32, parts[0].shape, 1) // width
    bit = count // 2
    while bit:
        low = (segment % (2 * bit)) < bit
        for a in range(count):
            if a & bit == 0:
                first, second = parts[a], parts[a + bit]
                parts[a] = jnp.where(low, first, pltpu.roll(second, bit * width, 1))
                parts[a + bit] = jnp.where(low, pltpu.roll(first, LANES - bit * width, 1), second)
        bit //= 2
    return parts


def kernel(
    rows,
    cols,
    a_hbm,
    pattern_ref,
    listed_ref,
    panel_hbm,
    link_hbm,
    diag_hbm,
    upper_ref,
    out_ref,
    a_ref,
    panel_ref,
    link_ref,
    diag_ref,
    panels,
    anc,
    slab,
    partial,
    shares,
    left_out,
    left_in,
    kept_out,
    kept_in,
    gather_out,
    gather_in,
    tile_out,
    tile_in,
    load_sems,
    anc_send,
    anc_recv,
    far_send,
    far_recv,
    sems,
):
    row, col = lax.axis_index("row"), lax.axis_index("col")
    depth = cols // 2
    z, side = lax.div(col, 2), lax.rem(col, 2)
    pair, core = lax.div(row, 2), lax.rem(row, 2)
    pairs = rows // 2
    height = panel_ref.shape[1]
    width = panel_ref.shape[2]
    half = width // 2
    plane = 2 * rows
    me = side * rows + row
    slot_me = (core * 2 + side) * pairs + pair
    tall = a_ref.shape[0]
    band_rows = width // rows
    band_cols = width // cols
    count = cols // 2
    own = lax.div(col, count) == side
    own_slab = lax.rem(lax.div(z, 2), 2) == lax.rem(pair, 2)

    (slab_sent, slab_got, left_sent, left_got, kept_sent, kept_got, share_sent, share_got) = (
        sems.at[i] for i in range(8)
    )
    gather_sent, gather_got, pass_sent, pass_got, tile_sent, tile_got = (sems.at[i] for i in range(8, 14))

    def wait_for(ref, sem):
        pltpu.make_async_copy(ref, ref, sem).wait()

    def place(index):
        return (lax.rem(index, rows), 2 * z + lax.div(index, rows))

    def peer(step):
        return lax.rem(me + step, plane)

    def plane_at(offset):
        return lax.rem(z + depth + offset, depth)

    def near(residue, core_from):
        gap = lax.rem(residue, 4)
        return jnp.where(gap == 3, -1, jnp.where(gap == 2, 2 - 4 * core_from, gap))

    loads = [
        pltpu.make_async_copy(panel_hbm, panel_ref, load_sems.at[0]),
        pltpu.make_async_copy(a_hbm, a_ref, load_sems.at[1]),
        pltpu.make_async_copy(diag_hbm, diag_ref, load_sems.at[2]),
        pltpu.make_async_copy(link_hbm, link_ref, load_sems.at[3]),
    ]
    with jax.named_scope("greet"):
        for load in loads:
            load.start()
        barrier = pltpu.get_barrier_semaphore()

        def greet(device):
            pl.semaphore_signal(barrier, inc=1, device_id=device, device_id_type=MESH)

        for far in (2, 1, 3):
            greet((row, lax.rem(col + 8 * far, cols)))

        @pl.loop(0, depth)
        def _(step):
            source = 2 * plane_at(step) + lax.div(col, count)

            @pl.when(source != col)
            def _():
                greet((row, source))

        @pl.loop(0, plane)
        def _(step):
            other = peer(step)
            row_from, side_from = lax.rem(other, rows), lax.div(other, rows)

            @pl.when(step > 0)
            def _():
                greet(place(other))

            for i in range(2):
                offset = near(z + depth - lax.rem(2 * pair + i, 4), lax.rem(row_from, 2))

                @pl.when(jnp.logical_or(step > 0, offset != 0))
                def _():
                    greet((row_from, 2 * plane_at(-offset) + side_from))

        def keep(s):
            found = listed_ref[s, 0] == col
            for i in range(1, listed_ref.shape[1]):
                found = jnp.logical_or(found, listed_ref[s, i] == col)
            return jnp.where(found, 1.0, 0.0).astype(F32)

        flag0, flag1 = keep(0), keep(1)
        loads[0].wait()
        kept0 = panel_ref[0] * flag0
        kept1 = panel_ref[1] * flag1
        panels[lax.div(z, 4), 0] = kept0
        panels[lax.div(z, 4), 1] = kept1
        loads[1].wait()
        for i in range(tall // BLK):
            present = pattern_ref[(tall // BLK) * row + i, col].astype(F32)
            anc[side, pl.ds(core * tall + i * BLK, BLK), :] = a_ref[pl.ds(i * BLK, BLK), :] * present
        slab_targets = 4 * rows - own_slab.astype(jnp.int32)
        tile_targets = count - own.astype(jnp.int32)
        pl.semaphore_wait(barrier, plane - 1 + 3 + slab_targets + tile_targets)

    def far_copy(j):
        piece = panels.at[lax.div(z, 4)]
        return pltpu.make_async_remote_copy(
            src_ref=piece,
            dst_ref=piece,
            send_sem=far_send.at[j - 1],
            recv_sem=far_recv.at[j - 1],
            device_id=(row, lax.rem(col + 8 * j, cols)),
            device_id_type=MESH,
        )

    def spread(j):
        block = plane_at(-4 * j)
        owner = lax.div(block, 2)
        slot = (lax.rem(block, 2) * 2 + side) * rows + row
        for offset in (2 - 4 * core, 1, -1, 0):
            for step in range(4):
                quarter = lax.rem(2 * core + side + step, 4)
                super_of, half_of = lax.div(quarter, 2), lax.rem(quarter, 2)
                source = panels.at[
                    lax.div(block, 4), super_of, :, pl.ds(pl.multiple_of(half_of * half, LANES), half)
                ]

                def send():
                    pltpu.make_async_remote_copy(
                        src_ref=source,
                        dst_ref=slab.at[slot],
                        send_sem=slab_sent,
                        recv_sem=slab_got,
                        device_id=(2 * owner + super_of, 2 * plane_at(offset) + half_of),
                        device_id_type=MESH,
                    ).start()

                if step == 0 and isinstance(offset, int) and offset == 0:
                    pl.when(owner != pair)(send)

                    @pl.when(owner == pair)
                    def _():
                        pltpu.make_async_copy(source, slab.at[slot], slab_got).start()
                else:
                    send()

    def anc_copy(i):
        other_row = 2 * pair + (core + i) % 2
        other_col = 2 * z + (side + i // 2) % 2
        piece = anc.at[side, pl.ds(core * tall, tall), :]
        return pltpu.make_async_remote_copy(
            src_ref=piece,
            dst_ref=piece,
            send_sem=anc_send.at[i - 1],
            recv_sem=anc_recv.at[i - 1],
            device_id=(other_row, other_col),
            device_id_type=MESH,
        )

    with jax.named_scope("start"):
        for j in (2, 1, 3):
            far_copy(j).start()
        for i in (1, 2, 3):
            anc_copy(i).start()
        spread(0)

    with jax.named_scope("early"):
        loads[2].wait()
        loads[3].wait()
        mixed = kept1 - dot(kept0, link_ref[...])
        link_band = link_ref[pl.ds(pl.multiple_of(row * band_rows, 8), band_rows), :]
        extra = dot(diag_ref[0], link_band)
        per = LANES // band_rows
        for g in range(width // LANES):
            cut = slice(g * LANES, (g + 1) * LANES)
            packed = exchange([kept0[:, cut], kept1[:, cut], mixed[:, cut], extra[:height, cut]], band_rows)
            for j in range(per):
                left_out[g * per + j, :, :LANES] = packed[j]
                tail = extra[height:, cut]
                if j:
                    tail = pltpu.roll(tail, LANES - j * band_rows, 1)
                left_out[g * per + j, :, LANES:] = tail
        for h in range(2):
            kept_out[h] = kept1[:, h * half : (h + 1) * half]
        left_in[slot_me] = left_out[row]
        kept_in[slot_me] = kept_out[side]

        @pl.loop(1, plane)
        def _(step):
            other = peer(step)
            target = place(other)
            pltpu.make_async_remote_copy(
                src_ref=left_out.at[target[0]],
                dst_ref=left_in.at[slot_me],
                send_sem=left_sent,
                recv_sem=left_got,
                device_id=target,
                device_id_type=MESH,
            ).start()
            pltpu.make_async_remote_copy(
                src_ref=kept_out.at[lax.div(other, rows)],
                dst_ref=kept_in.at[slot_me],
                send_sem=kept_sent,
                recv_sem=kept_got,
                device_id=target,
                device_id_type=MESH,
            ).start()

    with jax.named_scope("spread"):
        for j in (1, 3, 2):
            far_copy(j).wait_recv()
            spread(j)

    with jax.named_scope("slab"):
        for i in (1, 2, 3):
            anc_copy(i).wait_recv()
        wait_for(slab, slab_got)
    with jax.named_scope("product"):
        kept_rows = slab[...].reshape(2 * tall, half)
        for i in range(2):
            part = dot_rows(anc[i], kept_rows)
            partial[pl.ds(i * rows, rows)] = part.reshape(rows, height, half)

    slot = (2 * core + side) * pairs + pair
    with jax.named_scope("scatter"):
        shares[slot] = partial[me]

        @pl.loop(1, plane)
        def _(step):
            other = peer(step)
            pltpu.make_async_remote_copy(
                src_ref=partial.at[other],
                dst_ref=shares.at[slot],
                send_sem=share_sent,
                recv_sem=share_got,
                device_id=place(other),
                device_id_type=MESH,
            ).start()

    with jax.named_scope("linkterm"):
        wait_for(left_in.at[pl.ds(0, plane - 1)], left_got)
        wait_for(kept_in.at[pl.ds(0, plane - 1)], kept_got)
        lefts = left_in[...].reshape(plane * height, 2 * LANES)
        kept_half = kept_in[...].reshape(plane * height, half)
        column_half = pl.ds(pl.multiple_of(side * half, LANES), half)
        link_half = link_ref[:, column_half]
        group = pl.ds(pl.multiple_of(lax.div(row, per) * LANES, LANES), LANES)
        link_group = link_ref[:, group]
        link_rows = link_ref[pl.ds(pl.multiple_of(z * 2 * band_cols, 8), 2 * band_cols), column_half]

        def repeat(i):
            return jnp.concatenate(
                [
                    link_rows[s * band_cols + i : s * band_cols + i + height]
                    for _ in range(2)
                    for s in range(2)
                    for _ in range(pairs)
                ],
                axis=0,
            )

        constant = pltpu.roll(dot_rows(repeat(0), lefts[:, :LANES]), 2 * band_rows, 1) + pltpu.roll(
            dot_rows(repeat(height), lefts[:, LANES:]), band_rows, 1
        )

    with jax.named_scope("shares"):
        wait_for(shares.at[pl.ds(0, plane - 1)], share_got)
        quarters = []
        for q in range(4):
            total = shares[q * pairs]
            for i in range(1, pairs):
                total = total + shares[q * pairs + i]
            quarters.append(total)
        sum0 = jnp.concatenate(quarters[:2], axis=1)
        sum1 = jnp.concatenate(quarters[2:], axis=1)
        upper0 = -sum0 * flag0
        for h in range(2):
            gather_out[h, :, :width] = upper0
            gather_out[h, :, width:] = quarters[2 + h]
        gather_in[slot_me] = gather_out[side]

    with jax.named_scope("gather"):
        chip = side * pairs + pair

        @pl.loop(1, rows)
        def _(step):
            other = lax.rem(chip + step, rows)
            pltpu.make_async_remote_copy(
                src_ref=gather_out.at[lax.div(other, pairs)],
                dst_ref=gather_in.at[slot_me],
                send_sem=gather_sent,
                recv_sem=gather_got,
                device_id=(2 * lax.rem(other, pairs) + core, 2 * z + lax.div(other, pairs)),
                device_id_type=MESH,
            ).start()

        upper_ref[0] = upper0
        upper_ref[1] = -(sum1 + dot(upper0, link_ref[...])) * flag1
        wait_for(gather_in.at[pl.ds(0, rows - 1)], gather_got)
        mine = gather_in.at[pl.ds(core * rows, rows)]
        swap = pltpu.make_async_remote_copy(
            src_ref=mine,
            dst_ref=mine,
            send_sem=pass_sent,
            recv_sem=pass_got,
            device_id=(2 * pair + 1 - core, col),
            device_id_type=MESH,
        )
        swap.start()
        swap.wait_recv()

    with jax.named_scope("diagonal"):
        uppers = gather_in[:, :, :width].reshape(plane * height, width)
        sums = gather_in[:, :, width:].reshape(plane * height, half)
        chained_half = dot(uppers, link_half)
        chained_group = dot(uppers, link_group)
        upper_half = gather_in[:, :, column_half].reshape(plane * height, half)
        first = lefts[:, :LANES]
        turn = lax.rem(LANES + band_rows - lax.rem(row, per) * band_rows, LANES)
        later = (
            dot_rows(sums, first)
            + pltpu.roll(dot_rows(chained_half, first), LANES - band_rows, 1)
            + pltpu.roll(dot_rows(kept_half, chained_group), turn, 1)
            + constant
        )
        lane = lax.broadcasted_iota(jnp.int32, (half, LANES), 1)
        tiles = jnp.where(lane < band_rows, -dot_rows(upper_half, first), later)
        low = lane[:8] < 2 * band_rows
        for j in range(count):
            top = tiles[band_cols * j : band_cols * j + 8]
            bottom = tiles[band_cols * j + 8 : band_cols * j + 16]
            tile_out[j] = jnp.where(low, top, pltpu.roll(bottom, 2 * band_rows, 1))

    with jax.named_scope("tiles"):

        @pl.loop(0, count)
        def _(step):
            other = lax.rem(col + count // 2 + step, count)
            target = side * count + other

            @pl.when(target != col)
            def _():
                pltpu.make_async_remote_copy(
                    src_ref=tile_out.at[other],
                    dst_ref=tile_in.at[z],
                    send_sem=tile_sent,
                    recv_sem=tile_got,
                    device_id=(row, target),
                    device_id_type=MESH,
                ).start()

            @pl.when(target == col)
            def _():
                pltpu.make_async_copy(tile_out.at[other], tile_in.at[z], tile_got).start()

        wait_for(tile_in, tile_got)
        total = tile_in[0]
        for i in range(1, depth):
            total = total + tile_in[i]
        for i in range(2):
            for s in range(2):
                at = (2 * i + s) * band_rows
                out_ref[s, 8 * i : 8 * i + 8, :] = diag_ref[s, 8 * i : 8 * i + 8, :] + total[:, at : at + band_rows]

    with jax.named_scope("drain"):
        for i in (1, 2, 3):
            anc_copy(i).wait_send()
            far_copy(i).wait_send()

        @pl.when(own_slab)
        def _():
            wait_for(slab.at[pl.ds(0, 4 * rows - 1)], slab_sent)

        @pl.when(jnp.logical_not(own_slab))
        def _():
            wait_for(slab, slab_sent)

        wait_for(left_in.at[pl.ds(0, plane - 1)], left_sent)
        wait_for(kept_in.at[pl.ds(0, plane - 1)], kept_sent)
        wait_for(shares.at[pl.ds(0, plane - 1)], share_sent)
        wait_for(gather_in.at[pl.ds(0, rows - 1)], gather_sent)
        swap.wait_send()

        @pl.when(own)
        def _():
            wait_for(tile_in.at[pl.ds(0, count - 1)], tile_sent)

        @pl.when(jnp.logical_not(own))
        def _():
            wait_for(tile_in, tile_sent)


def local(rows, cols, ancestor_inverse, pattern, listed, panels, parent_panels, diag_inverse):
    supers, height, width = panels.shape
    tall, wide = ancestor_inverse.shape
    depth = cols // 2
    plane = 2 * rows
    half = width // 2
    count = cols // 2
    vmem = pl.BlockSpec(memory_space=pltpu.VMEM)
    smem = pl.BlockSpec(memory_space=pltpu.SMEM)
    anywhere = pl.BlockSpec(memory_space=pl.ANY)
    turned = jnp.swapaxes(diag_inverse, 1, 2)
    upper, tiles = pl.pallas_call(
        functools.partial(kernel, rows, cols),
        out_shape=(
            jax.ShapeDtypeStruct(panels.shape, F32),
            jax.ShapeDtypeStruct(turned.shape, F32),
        ),
        in_specs=[anywhere, smem, smem, anywhere, anywhere, anywhere],
        out_specs=(vmem, vmem),
        scratch_shapes=[
            pltpu.VMEM(ancestor_inverse.shape, F32),
            pltpu.VMEM(panels.shape, F32),
            pltpu.VMEM((width, width), F32),
            pltpu.VMEM(turned.shape, F32),
            pltpu.VMEM((depth // 4, supers, height, width), F32),
            pltpu.VMEM((2, 2 * tall, wide), F32),
            pltpu.VMEM((4 * rows, height, half), F32),
            pltpu.VMEM((plane, height, half), F32),
            pltpu.VMEM((plane, height, half), F32),
            pltpu.VMEM((rows, height, 2 * LANES), F32),
            pltpu.VMEM((plane, height, 2 * LANES), F32),
            pltpu.VMEM((2, height, half), F32),
            pltpu.VMEM((plane, height, half), F32),
            pltpu.VMEM((2, height, width + half), F32),
            pltpu.VMEM((plane, height, width + half), F32),
            pltpu.VMEM((count, 8, LANES), F32),
            pltpu.VMEM((depth, 8, LANES), F32),
            pltpu.SemaphoreType.DMA((4,)),
            pltpu.SemaphoreType.DMA((3,)),
            pltpu.SemaphoreType.DMA((3,)),
            pltpu.SemaphoreType.DMA((3,)),
            pltpu.SemaphoreType.DMA((3,)),
            pltpu.SemaphoreType.DMA((14,)),
        ],
        compiler_params=pltpu.CompilerParams(
            collective_id=0, has_side_effects=True, vmem_limit_bytes=56 * 1024 * 1024
        ),
    )(ancestor_inverse, pattern, listed, panels, parent_panels[0], turned)
    return upper, jnp.swapaxes(tiles, 1, 2)


def solution(mesh):
    rows, cols = mesh.shape["row"], mesh.shape["col"]
    return jax.shard_map(
        functools.partial(local, rows, cols),
        mesh=mesh,
        in_specs=(
            P("row", "col"),
            P(),
            P(),
            P(None, ("col", "row"), None),
            P(),
            P(None, "row", "col"),
        ),
        out_specs=(P(None, ("col", "row"), None), P(None, "row", "col")),
        check_vma=False,
    )
```

```python
import functools

import jax
import jax.numpy as jnp
from jax import lax
from jax.experimental import pallas as pl
from jax.experimental.pallas import tpu as pltpu
from jax.sharding import PartitionSpec as P

BLK = 128
LANES = 128
STRIDE = 5
MESH = pl.DeviceIdType.MESH
F32 = jnp.float32


def dot(left, right):
    return jnp.dot(left, right, precision=lax.Precision.HIGHEST, preferred_element_type=F32)


def dot_rows(left, right):
    return lax.dot_general(
        left,
        right,
        (((0,), (0,)), ((), ())),
        precision=lax.Precision.HIGHEST,
        preferred_element_type=F32,
    )


def split(value):
    high = value.astype(jnp.bfloat16)
    return high, (value - high.astype(F32)).astype(jnp.bfloat16)


def dot_split(left, right, dim=1):
    def once(a, b):
        return lax.dot_general(a, b, (((dim,), (0,)), ((), ())), preferred_element_type=F32)

    return once(left[0], right[1]) + once(left[1], right[0]) + once(left[0], right[0])


def exchange(parts, width):
    parts = list(parts)
    count = len(parts)
    segment = lax.broadcasted_iota(jnp.int32, parts[0].shape, 1) // width
    bit = count // 2
    while bit:
        low = (segment % (2 * bit)) < bit
        for a in range(count):
            if a & bit == 0:
                first, second = parts[a], parts[a + bit]
                parts[a] = jnp.where(low, first, pltpu.roll(second, bit * width, 1))
                parts[a + bit] = jnp.where(low, pltpu.roll(first, LANES - bit * width, 1), second)
        bit //= 2
    return parts


def kernel(
    rows,
    cols,
    a_hbm,
    pattern_ref,
    listed_ref,
    panel_hbm,
    link_hbm,
    diag_hbm,
    upper_ref,
    out_ref,
    a_ref,
    panel_ref,
    link_ref,
    diag_ref,
    panels,
    anc,
    slab,
    partial,
    shares,
    left_out,
    left_in,
    kept_out,
    kept_in,
    gather_out,
    gather_in,
    tile_out,
    tile_in,
    extra_out,
    extra_in,
    load_sems,
    anc_send,
    anc_recv,
    far_send,
    far_recv,
    gather_got,
    sems,
):
    row, col = lax.axis_index("row"), lax.axis_index("col")
    depth = cols // 2
    z, side = lax.div(col, 2), lax.rem(col, 2)
    pair, core = lax.div(row, 2), lax.rem(row, 2)
    pairs = rows // 2
    height = panel_ref.shape[1]
    width = panel_ref.shape[2]
    half = width // 2
    plane = 2 * rows
    me = side * rows + row
    slot_me = (core * 2 + side) * pairs + pair
    tall = a_ref.shape[0]
    band_rows = width // rows
    band_cols = width // cols
    count = cols // 2
    own = lax.div(col, count) == side

    (slab_sent, slab_got, left_sent, left_got, kept_sent, kept_got, share_sent, share_got) = (
        sems.at[i] for i in range(8)
    )
    gather_sent, pass_sent, pass_got, tile_sent, tile_got = (sems.at[i] for i in range(8, 13))
    extra_sent, extra_got, forward_sent, forward_got = (sems.at[i] for i in range(13, 17))

    def wait_for(ref, sem):
        pltpu.make_async_copy(ref, ref, sem).wait()

    def place(index):
        return (lax.rem(index, rows), 2 * z + lax.div(index, rows))

    def peer(step):
        return lax.rem(me + step, plane)

    def plane_at(offset):
        return lax.rem(z + depth + offset, depth)

    def holder(block):
        gap = lax.rem(z + depth - block, depth)
        back = jnp.where(gap <= 2, 0, jnp.where(gap <= depth // 2, STRIDE, depth - STRIDE))
        back = jnp.where(gap >= depth - 2, 0, back)
        return lax.rem(block + back, depth)

    held = [(0, (2, -2, 1, -1, 0)), (-STRIDE, (3, 2, -2, 1, -1, 0)), (STRIDE, (2, -2, 1, -1, 0))]
    own_slab = functools.reduce(jnp.logical_or, [lax.div(plane_at(offset), 2) == pair for offset, _ in held])

    loads = [
        pltpu.make_async_copy(panel_hbm, panel_ref, load_sems.at[0]),
        pltpu.make_async_copy(a_hbm, a_ref, load_sems.at[1]),
        pltpu.make_async_copy(diag_hbm, diag_ref, load_sems.at[2]),
        pltpu.make_async_copy(link_hbm, link_ref, load_sems.at[3]),
    ]
    with jax.named_scope("greet"):
        for load in loads:
            load.start()
        barrier = pltpu.get_barrier_semaphore()

        def greet(device):
            pl.semaphore_signal(barrier, inc=1, device_id=device, device_id_type=MESH)

        for far in (STRIDE, -STRIDE):
            greet((row, lax.rem(col + cols + 2 * far, cols)))

        @pl.loop(0, plane)
        def _(step):
            other = peer(step)
            row_from, side_from = lax.rem(other, rows), lax.div(other, rows)
            for i in range(2):
                source = holder(2 * pair + i)

                @pl.when(jnp.logical_or(step > 0, source != z))
                def _():
                    greet((row_from, 2 * source + side_from))

        @pl.loop(1, plane)
        def _(step):
            greet(place(peer(step)))

        def keep(s):
            found = listed_ref[s, 0] == col
            for i in range(1, listed_ref.shape[1]):
                found = jnp.logical_or(found, listed_ref[s, i] == col)
            return jnp.where(found, 1.0, 0.0).astype(F32)

        flag0, flag1 = keep(0), keep(1)
        loads[0].wait()
        kept0 = panel_ref[0] * flag0
        kept1 = panel_ref[1] * flag1
        panels[0, 0] = kept0
        panels[0, 1] = kept1
        loads[1].wait()
        for i in range(tall // BLK):
            present = pattern_ref[(tall // BLK) * row + i, col].astype(F32)
            anc[side, pl.ds(core * tall + i * BLK, BLK), :] = a_ref[pl.ds(i * BLK, BLK), :] * present
        for h in range(2):
            kept_out[h] = kept1[:, h * half : (h + 1) * half]
        kept_in[slot_me] = kept_out[side]
        loads[2].wait()
        loads[3].wait()
        mixed = kept1 - dot(kept0, link_ref[...])
        link_band = link_ref[pl.ds(pl.multiple_of(row * band_rows, 8), band_rows), :]
        extra = dot(diag_ref[0], link_band)
        for h in range(2):
            extra_out[h] = extra[h * height : (h + 1) * height]
        slab_targets = 4 * rows - own_slab.astype(jnp.int32)
        pl.semaphore_wait(barrier, plane - 1 + 2 + slab_targets)

    def far_copy(j):
        return pltpu.make_async_remote_copy(
            src_ref=panels.at[0],
            dst_ref=panels.at[j],
            send_sem=far_send.at[j - 1],
            recv_sem=far_recv.at[j - 1],
            device_id=(row, lax.rem(col + cols + (2 * STRIDE if j == 1 else -2 * STRIDE), cols)),
            device_id_type=MESH,
        )

    def spread(j):
        back, offsets = held[j]
        block = plane_at(back)
        owner = lax.div(block, 2)
        slot = (lax.rem(block, 2) * 2 + side) * rows + row
        for offset in offsets:
            for step in range(4):
                quarter = lax.rem(2 * core + side + step, 4)
                super_of, half_of = lax.div(quarter, 2), lax.rem(quarter, 2)
                source = panels.at[j, super_of, :, pl.ds(pl.multiple_of(half_of * half, LANES), half)]

                def send():
                    pltpu.make_async_remote_copy(
                        src_ref=source,
                        dst_ref=slab.at[slot],
                        send_sem=slab_sent,
                        recv_sem=slab_got,
                        device_id=(2 * owner + super_of, 2 * plane_at(offset) + half_of),
                        device_id_type=MESH,
                    ).start()

                if step == 0 and offset == 0:
                    pl.when(owner != pair)(send)

                    @pl.when(owner == pair)
                    def _():
                        pltpu.make_async_copy(source, slab.at[slot], slab_got).start()
                else:
                    send()

    def anc_copy(i):
        other_row = 2 * pair + (core + i) % 2
        other_col = 2 * z + (side + i // 2) % 2
        piece = anc.at[side, pl.ds(core * tall, tall), :]
        return pltpu.make_async_remote_copy(
            src_ref=piece,
            dst_ref=piece,
            send_sem=anc_send.at[i - 1],
            recv_sem=anc_recv.at[i - 1],
            device_id=(other_row, other_col),
            device_id_type=MESH,
        )

    def chip_copy(source, target, sent, got):
        return pltpu.make_async_remote_copy(
            src_ref=source,
            dst_ref=target,
            send_sem=sent,
            recv_sem=got,
            device_id=(2 * pair + 1 - core, col),
            device_id_type=MESH,
        )

    chip = side * pairs + pair

    def chip_at(step):
        other = lax.rem(chip + step, rows)
        return lax.div(other, pairs), (2 * lax.rem(other, pairs) + core, 2 * z + lax.div(other, pairs))

    with jax.named_scope("start"):
        for j in (1, 2):
            far_copy(j).start()
        extra_swap = chip_copy(extra_out.at[1 - core], extra_in, extra_sent, extra_got)
        extra_swap.start()
        for i in (1, 2, 3):
            anc_copy(i).start()
        spread(0)

    with jax.named_scope("early"):

        @pl.loop(1, rows)
        def _(step):
            side_to, target = chip_at(step)
            pltpu.make_async_remote_copy(
                src_ref=kept_out.at[side_to],
                dst_ref=kept_in.at[slot_me],
                send_sem=kept_sent,
                recv_sem=kept_got,
                device_id=target,
                device_id_type=MESH,
            ).start()

        extra_swap.wait_recv()
        extra = extra_out[core] + extra_in[...]
        per = LANES // band_rows
        for g in range(width // LANES):
            cut = slice(g * LANES, (g + 1) * LANES)
            packed = exchange([kept0[:, cut], kept1[:, cut], mixed[:, cut], extra[:, cut]], band_rows)
            for j in range(per):
                left_out[g * per + j] = packed[j]
        left_in[slot_me] = left_out[row]

        @pl.loop(1, plane)
        def _(step):
            target = place(peer(step))
            pltpu.make_async_remote_copy(
                src_ref=left_out.at[target[0]],
                dst_ref=left_in.at[slot_me],
                send_sem=left_sent,
                recv_sem=left_got,
                device_id=target,
                device_id_type=MESH,
            ).start()

    with jax.named_scope("spread"):
        for j in (1, 2):
            far_copy(j).wait_recv()
            spread(j)

    with jax.named_scope("slab"):
        for i in (1, 2, 3):
            anc_copy(i).wait_recv()
        wait_for(slab, slab_got)
    with jax.named_scope("product"):
        kept_rows = split(slab[...].reshape(2 * tall, half))
        for i in range(2):
            part = dot_split(split(anc[i]), kept_rows, 0)
            partial[pl.ds(i * rows, rows)] = part.reshape(rows, height, half)

    slot = (2 * core + side) * pairs + pair
    with jax.named_scope("scatter"):
        shares[slot] = partial[me]

        @pl.loop(1, plane)
        def _(step):
            other = peer(step)
            pltpu.make_async_remote_copy(
                src_ref=partial.at[other],
                dst_ref=shares.at[slot],
                send_sem=share_sent,
                recv_sem=share_got,
                device_id=place(other),
                device_id_type=MESH,
            ).start()

    with jax.named_scope("linkterm"):
        wait_for(kept_in.at[pl.ds(0, rows - 1)], kept_got)
        mine = pl.ds(core * rows, rows)
        kept_swap = chip_copy(kept_in.at[mine], kept_in.at[mine], forward_sent, forward_got)
        kept_swap.start()
        wait_for(left_in.at[pl.ds(0, plane - 1)], left_got)
        lefts = left_in[...].reshape(plane * height, LANES)
        column_half = pl.ds(pl.multiple_of(side * half, LANES), half)
        group = pl.ds(pl.multiple_of(lax.div(row, per) * LANES, LANES), LANES)
        link_half = split(link_ref[:, column_half])
        link_group = split(link_ref[:, group])
        link_rows = link_ref[pl.ds(pl.multiple_of(z * 2 * band_cols, 8), 2 * band_cols), column_half]
        repeated = jnp.concatenate(
            [
                link_rows[s * band_cols + k * height : s * band_cols + (k + 1) * height]
                for k in range(2)
                for s in range(2)
                for _ in range(pairs)
            ],
            axis=0,
        )
        constant = pltpu.roll(dot_rows(repeated, lefts), 2 * band_rows, 1)
        first = split(lefts)
        kept_swap.wait_recv()
        kept_half = split(kept_in[...].reshape(plane * height, half))

    with jax.named_scope("shares"):
        wait_for(shares.at[pl.ds(0, plane - 1)], share_got)
        quarters = []
        for q in range(4):
            total = shares[q * pairs]
            for i in range(1, pairs):
                total = total + shares[q * pairs + i]
            quarters.append(total)
        sum0 = jnp.concatenate(quarters[:2], axis=1)
        sum1 = jnp.concatenate(quarters[2:], axis=1)
        upper0 = -sum0 * flag0
        for h in range(2):
            gather_out[h, :, :width] = upper0
            gather_out[h, :, width:] = quarters[2 + h]
        gather_in[slot_me] = gather_out[side]

    with jax.named_scope("gather"):

        @pl.loop(1, rows)
        def _(step):
            side_to, target = chip_at(step)
            pltpu.make_async_remote_copy(
                src_ref=gather_out.at[side_to],
                dst_ref=gather_in.at[slot_me],
                send_sem=gather_sent,
                recv_sem=gather_got.at[step],
                device_id=target,
                device_id_type=MESH,
            ).start()

        chip_copy(gather_in.at[slot_me], gather_in.at[slot_me], pass_sent, pass_got).start()
        upper_ref[0] = upper0
        upper_ref[1] = -(sum1 + dot(upper0, link_ref[...])) * flag1

        @pl.loop(1, rows)
        def _(step):
            slot_from = core * rows + lax.rem(chip + rows - step, rows)
            arrived = gather_in.at[slot_from]
            wait_for(arrived, gather_got.at[step])
            chip_copy(arrived, arrived, pass_sent, pass_got).start()

        wait_for(gather_in.at[mine], pass_got)

    with jax.named_scope("diagonal"):
        uppers = split(gather_in[:, :, :width].reshape(plane * height, width))
        sums = split(gather_in[:, :, width:].reshape(plane * height, half))
        chained_half = split(dot_split(uppers, link_half))
        chained_group = split(dot_split(uppers, link_group))
        upper_half = split(gather_in[:, :, column_half].reshape(plane * height, half))
        turn = lax.rem(LANES + band_rows - lax.rem(row, per) * band_rows, LANES)
        later = (
            dot_split(sums, first, 0)
            + pltpu.roll(dot_split(chained_half, first, 0), LANES - band_rows, 1)
            + pltpu.roll(dot_split(kept_half, chained_group, 0), turn, 1)
            + constant
        )
        lane = lax.broadcasted_iota(jnp.int32, (half, LANES), 1)
        tiles = jnp.where(lane < band_rows, -dot_split(upper_half, first, 0), later)
        low = lane[:8] < 2 * band_rows
        for j in range(count):
            top = tiles[band_cols * j : band_cols * j + 8]
            bottom = tiles[band_cols * j + 8 : band_cols * j + 16]
            tile_out[j] = jnp.where(low, top, pltpu.roll(bottom, 2 * band_rows, 1))

    with jax.named_scope("tiles"):

        @pl.loop(0, count)
        def _(step):
            other = lax.rem(col + count // 2 + step, count)
            target = side * count + other

            @pl.when(target != col)
            def _():
                pltpu.make_async_remote_copy(
                    src_ref=tile_out.at[other],
                    dst_ref=tile_in.at[z],
                    send_sem=tile_sent,
                    recv_sem=tile_got,
                    device_id=(row, target),
                    device_id_type=MESH,
                ).start()

            @pl.when(target == col)
            def _():
                pltpu.make_async_copy(tile_out.at[other], tile_in.at[z], tile_got).start()

        wait_for(tile_in, tile_got)
        total = tile_in[0]
        for i in range(1, depth):
            total = total + tile_in[i]
        for i in range(2):
            for s in range(2):
                at = (2 * i + s) * band_rows
                out_ref[s, 8 * i : 8 * i + 8, :] = diag_ref[s, 8 * i : 8 * i + 8, :] + total[:, at : at + band_rows]

    with jax.named_scope("drain"):
        for i in (1, 2, 3):
            anc_copy(i).wait_send()
        for j in (1, 2):
            far_copy(j).wait_send()
        extra_swap.wait_send()
        kept_swap.wait_send()

        @pl.when(own_slab)
        def _():
            wait_for(slab.at[pl.ds(0, 4 * rows - 1)], slab_sent)

        @pl.when(jnp.logical_not(own_slab))
        def _():
            wait_for(slab, slab_sent)

        wait_for(left_in.at[pl.ds(0, plane - 1)], left_sent)
        wait_for(kept_in.at[pl.ds(0, rows - 1)], kept_sent)
        wait_for(shares.at[pl.ds(0, plane - 1)], share_sent)
        wait_for(gather_in.at[pl.ds(0, rows - 1)], gather_sent)
        wait_for(gather_in.at[mine], pass_sent)

        @pl.when(own)
        def _():
            wait_for(tile_in.at[pl.ds(0, count - 1)], tile_sent)

        @pl.when(jnp.logical_not(own))
        def _():
            wait_for(tile_in, tile_sent)


def local(rows, cols, ancestor_inverse, pattern, listed, panels, parent_panels, diag_inverse):
    supers, height, width = panels.shape
    tall, wide = ancestor_inverse.shape
    depth = cols // 2
    plane = 2 * rows
    half = width // 2
    count = cols // 2
    vmem = pl.BlockSpec(memory_space=pltpu.VMEM)
    smem = pl.BlockSpec(memory_space=pltpu.SMEM)
    anywhere = pl.BlockSpec(memory_space=pl.ANY)
    turned = jnp.swapaxes(diag_inverse, 1, 2)
    upper, tiles = pl.pallas_call(
        functools.partial(kernel, rows, cols),
        out_shape=(
            jax.ShapeDtypeStruct(panels.shape, F32),
            jax.ShapeDtypeStruct(turned.shape, F32),
        ),
        in_specs=[anywhere, smem, smem, anywhere, anywhere, anywhere],
        out_specs=(vmem, vmem),
        scratch_shapes=[
            pltpu.VMEM(ancestor_inverse.shape, F32),
            pltpu.VMEM(panels.shape, F32),
            pltpu.VMEM((width, width), F32),
            pltpu.VMEM(turned.shape, F32),
            pltpu.VMEM((3, supers, height, width), F32),
            pltpu.VMEM((2, 2 * tall, wide), F32),
            pltpu.VMEM((4 * rows, height, half), F32),
            pltpu.VMEM((plane, height, half), F32),
            pltpu.VMEM((plane, height, half), F32),
            pltpu.VMEM((rows, height, LANES), F32),
            pltpu.VMEM((plane, height, LANES), F32),
            pltpu.VMEM((2, height, half), F32),
            pltpu.VMEM((plane, height, half), F32),
            pltpu.VMEM((2, height, width + half), F32),
            pltpu.VMEM((plane, height, width + half), F32),
            pltpu.VMEM((count, 8, LANES), F32),
            pltpu.VMEM((depth, 8, LANES), F32),
            pltpu.VMEM((2, height, width), F32),
            pltpu.VMEM((height, width), F32),
            pltpu.SemaphoreType.DMA((4,)),
            pltpu.SemaphoreType.DMA((3,)),
            pltpu.SemaphoreType.DMA((3,)),
            pltpu.SemaphoreType.DMA((2,)),
            pltpu.SemaphoreType.DMA((2,)),
            pltpu.SemaphoreType.DMA((rows,)),
            pltpu.SemaphoreType.DMA((17,)),
        ],
        compiler_params=pltpu.CompilerParams(
            collective_id=0, has_side_effects=True, vmem_limit_bytes=56 * 1024 * 1024
        ),
    )(ancestor_inverse, pattern, listed, panels, parent_panels[0], turned)
    return upper, jnp.swapaxes(tiles, 1, 2)


def solution(mesh):
    rows, cols = mesh.shape["row"], mesh.shape["col"]
    return jax.shard_map(
        functools.partial(local, rows, cols),
        mesh=mesh,
        in_specs=(
            P("row", "col"),
            P(),
            P(),
            P(None, ("col", "row"), None),
            P(),
            P(None, "row", "col"),
        ),
        out_specs=(P(None, ("col", "row"), None), P(None, "row", "col")),
        check_vma=False,
    )
```

```python
import functools

import jax
import jax.numpy as jnp
from jax import lax
from jax.experimental import pallas as pl
from jax.experimental.pallas import tpu as pltpu
from jax.sharding import PartitionSpec as P

BLK = 128
LANES = 128
STRIDE = 5
HOPS = (3, 2, -2, 1, -1)
MESH = pl.DeviceIdType.MESH
F32 = jnp.float32


def dot(left, right):
    return jnp.dot(left, right, precision=lax.Precision.HIGHEST, preferred_element_type=F32)


def dot_rows(left, right):
    return lax.dot_general(
        left,
        right,
        (((0,), (0,)), ((), ())),
        precision=lax.Precision.HIGHEST,
        preferred_element_type=F32,
    )


def split(value):
    high = value.astype(jnp.bfloat16)
    return high, (value - high.astype(F32)).astype(jnp.bfloat16)


def dot_split(left, right, dim=1):
    def once(a, b):
        return lax.dot_general(a, b, (((dim,), (0,)), ((), ())), preferred_element_type=F32)

    return once(left[0], right[1]) + once(left[1], right[0]) + once(left[0], right[0])


def exchange(parts, width):
    parts = list(parts)
    count = len(parts)
    segment = lax.broadcasted_iota(jnp.int32, parts[0].shape, 1) // width
    bit = count // 2
    while bit:
        low = (segment % (2 * bit)) < bit
        for a in range(count):
            if a & bit == 0:
                first, second = parts[a], parts[a + bit]
                parts[a] = jnp.where(low, first, pltpu.roll(second, bit * width, 1))
                parts[a + bit] = jnp.where(low, pltpu.roll(first, LANES - bit * width, 1), second)
        bit //= 2
    return parts


def kernel(
    rows,
    cols,
    a_hbm,
    pattern_ref,
    listed_ref,
    panel_hbm,
    link_hbm,
    diag_hbm,
    upper_ref,
    out_ref,
    a_ref,
    panel_ref,
    link_ref,
    diag_ref,
    panels,
    anc,
    slab,
    partial,
    shares,
    left_out,
    left_in,
    kept_out,
    kept_in,
    gather_out,
    gather_in,
    tile_out,
    tile_in,
    extra_out,
    extra_in,
    load_sems,
    anc_send,
    anc_recv,
    far_send,
    far_recv,
    gather_got,
    ready,
    sems,
):
    row, col = lax.axis_index("row"), lax.axis_index("col")
    depth = cols // 2
    z, side = lax.div(col, 2), lax.rem(col, 2)
    pair, core = lax.div(row, 2), lax.rem(row, 2)
    pairs = rows // 2
    height = panel_ref.shape[1]
    width = panel_ref.shape[2]
    half = width // 2
    plane = 2 * rows
    me = side * rows + row
    slot_me = (core * 2 + side) * pairs + pair
    tall = a_ref.shape[0]
    band_rows = width // rows
    band_cols = width // cols
    count = cols // 2
    own = lax.div(col, count) == side

    (slab_sent, slab_got, left_sent, left_got, kept_sent, kept_got, share_sent, share_got) = (
        sems.at[i] for i in range(8)
    )
    gather_sent, pass_sent, pass_got, tile_sent, tile_got = (sems.at[i] for i in range(8, 13))
    extra_sent, extra_got, forward_sent, forward_got = (sems.at[i] for i in range(13, 17))

    def wait_for(ref, sem):
        pltpu.make_async_copy(ref, ref, sem).wait()

    def wrap(value, size):
        return jnp.where(value >= size, value - size, value)

    def plane_at(offset):
        return wrap(z + offset % depth, depth)

    def each_peer(act):
        act(row, 1 - side)

        @pl.loop(1, rows)
        def _(step):
            other = wrap(row + step, rows)
            act(other, side)
            act(other, 1 - side)

    def each_chip(act):
        act(pair, 1 - side, 1)

        @pl.loop(1, pairs)
        def _(step):
            other = wrap(pair + step, pairs)
            act(other, side, 2 * step)
            act(other, 1 - side, 2 * step + 1)

    held = [(0, (*HOPS[1:], 0)), (-STRIDE, (*HOPS, 0)), (STRIDE, (*HOPS[1:], 0))]
    own_slab = functools.reduce(jnp.logical_or, [lax.div(plane_at(offset), 2) == pair for offset, _ in held])

    loads = [
        pltpu.make_async_copy(panel_hbm, panel_ref, load_sems.at[0]),
        pltpu.make_async_copy(a_hbm, a_ref, load_sems.at[1]),
        pltpu.make_async_copy(diag_hbm, diag_ref, load_sems.at[2]),
        pltpu.make_async_copy(link_hbm, link_ref, load_sems.at[3]),
    ]
    with jax.named_scope("greet"):
        for load in loads:
            load.start()
        barrier = pltpu.get_barrier_semaphore()

        def greet(device):
            pl.semaphore_signal(barrier, inc=1, device_id=device, device_id_type=MESH)

        for offset in (*HOPS, STRIDE, -STRIDE):
            greet((row, 2 * plane_at(offset) + side))
        each_peer(lambda r, s: greet((r, 2 * z + s)))

        def keep(s):
            found = listed_ref[s, 0] == col
            for i in range(1, listed_ref.shape[1]):
                found = jnp.logical_or(found, listed_ref[s, i] == col)
            return jnp.where(found, 1.0, 0.0).astype(F32)

        flag0, flag1 = keep(0), keep(1)
        loads[0].wait()
        kept0 = panel_ref[0] * flag0
        kept1 = panel_ref[1] * flag1
        panels[0, 0] = kept0
        panels[0, 1] = kept1
        loads[1].wait()
        for i in range(tall // BLK):
            present = pattern_ref[(tall // BLK) * row + i, col].astype(F32)
            anc[side, pl.ds(core * tall + i * BLK, BLK), :] = a_ref[pl.ds(i * BLK, BLK), :] * present
        pl.semaphore_wait(barrier, plane - 1 + len(HOPS) + 2)

    def far_copy(j):
        return pltpu.make_async_remote_copy(
            src_ref=panels.at[0],
            dst_ref=panels.at[j],
            send_sem=far_send.at[j - 1],
            recv_sem=far_recv.at[j - 1],
            device_id=(row, 2 * plane_at(STRIDE if j == 1 else -STRIDE) + side),
            device_id_type=MESH,
        )

    def spread(j):
        back, offsets = held[j]
        block = plane_at(back)
        owner = lax.div(block, 2)
        slot = (lax.rem(block, 2) * 2 + side) * rows + row
        for offset in offsets:
            for step in range(4):
                super_of = core if step < 2 else 1 - core
                half_of = side if step % 2 == 0 else 1 - side
                source = panels.at[j, super_of, :, pl.ds(pl.multiple_of(half_of * half, LANES), half)]

                def send():
                    pltpu.make_async_remote_copy(
                        src_ref=source,
                        dst_ref=slab.at[slot],
                        send_sem=slab_sent,
                        recv_sem=slab_got,
                        device_id=(2 * owner + super_of, 2 * plane_at(offset) + half_of),
                        device_id_type=MESH,
                    ).start()

                if step == 0 and offset == 0:
                    pl.when(owner != pair)(send)

                    @pl.when(owner == pair)
                    def _():
                        pltpu.make_async_copy(source, slab.at[slot], slab_got).start()
                else:
                    send()

    def anc_copy(i):
        other_row = row if i == 2 else 2 * pair + 1 - core
        other_col = col if i == 1 else 2 * z + 1 - side
        piece = anc.at[side, pl.ds(core * tall, tall), :]
        return pltpu.make_async_remote_copy(
            src_ref=piece,
            dst_ref=piece,
            send_sem=anc_send.at[i - 1],
            recv_sem=anc_recv.at[i - 1],
            device_id=(other_row, other_col),
            device_id_type=MESH,
        )

    def chip_copy(source, target, sent, got):
        return pltpu.make_async_remote_copy(
            src_ref=source,
            dst_ref=target,
            send_sem=sent,
            recv_sem=got,
            device_id=(2 * pair + 1 - core, col),
            device_id_type=MESH,
        )

    with jax.named_scope("start"):
        for j in (1, 2):
            far_copy(j).start()
        for offset in HOPS:
            pl.semaphore_signal(
                ready, inc=1, device_id=(row, 2 * plane_at(-offset) + side), device_id_type=MESH
            )
        for i in (1, 2, 3):
            anc_copy(i).start()

    with jax.named_scope("early"):
        for h in range(2):
            kept_out[h] = kept1[:, h * half : (h + 1) * half]
        kept_in[slot_me] = kept_out[side]

        def send_kept(p, s, _):
            pltpu.make_async_remote_copy(
                src_ref=kept_out.at[s],
                dst_ref=kept_in.at[slot_me],
                send_sem=kept_sent,
                recv_sem=kept_got,
                device_id=(2 * p + core, 2 * z + s),
                device_id_type=MESH,
            ).start()

        loads[2].wait()
        loads[3].wait()
        mixed = kept1 - dot(kept0, link_ref[...])
        link_band = link_ref[pl.ds(pl.multiple_of(row * band_rows, 8), band_rows), :]
        extra = dot(diag_ref[0], link_band)
        for h in range(2):
            extra_out[h] = extra[h * height : (h + 1) * height]
        extra_swap = chip_copy(extra_out.at[1 - core], extra_in, extra_sent, extra_got)
        extra_swap.start()
        pl.semaphore_wait(ready, len(HOPS))
        spread(0)
        each_chip(send_kept)
        extra_swap.wait_recv()
        extra = extra_out[core] + extra_in[...]
        per = LANES // band_rows
        for g in range(width // LANES):
            cut = slice(g * LANES, (g + 1) * LANES)
            packed = exchange([kept0[:, cut], kept1[:, cut], mixed[:, cut], extra[:, cut]], band_rows)
            for j in range(per):
                left_out[g * per + j] = packed[j]
        left_in[slot_me] = left_out[row]

        @each_peer
        def _(r, s):
            pltpu.make_async_remote_copy(
                src_ref=left_out.at[r],
                dst_ref=left_in.at[slot_me],
                send_sem=left_sent,
                recv_sem=left_got,
                device_id=(r, 2 * z + s),
                device_id_type=MESH,
            ).start()

    with jax.named_scope("spread"):
        for j in (1, 2):
            far_copy(j).wait_recv()
            spread(j)

    with jax.named_scope("slab"):
        for i in (1, 2, 3):
            anc_copy(i).wait_recv()
        wait_for(slab, slab_got)
    with jax.named_scope("product"):
        kept_rows = split(slab[...].reshape(2 * tall, half))
        for i in range(2):
            part = dot_split(split(anc[i]), kept_rows, 0)
            partial[pl.ds(i * rows, rows)] = part.reshape(rows, height, half)

    slot = (2 * core + side) * pairs + pair
    with jax.named_scope("scatter"):
        shares[slot] = partial[me]

        @each_peer
        def _(r, s):
            pltpu.make_async_remote_copy(
                src_ref=partial.at[s * rows + r],
                dst_ref=shares.at[slot],
                send_sem=share_sent,
                recv_sem=share_got,
                device_id=(r, 2 * z + s),
                device_id_type=MESH,
            ).start()

    with jax.named_scope("linkterm"):
        wait_for(kept_in.at[pl.ds(0, rows - 1)], kept_got)
        mine = pl.ds(core * rows, rows)
        kept_swap = chip_copy(kept_in.at[mine], kept_in.at[mine], forward_sent, forward_got)
        kept_swap.start()
        wait_for(left_in.at[pl.ds(0, plane - 1)], left_got)
        lefts = left_in[...].reshape(plane * height, LANES)
        column_half = pl.ds(pl.multiple_of(side * half, LANES), half)
        group = pl.ds(pl.multiple_of(lax.div(row, per) * LANES, LANES), LANES)
        link_half = split(link_ref[:, column_half])
        link_group = split(link_ref[:, group])
        link_rows = link_ref[pl.ds(pl.multiple_of(z * 2 * band_cols, 8), 2 * band_cols), column_half]
        repeated = jnp.concatenate(
            [
                link_rows[s * band_cols + k * height : s * band_cols + (k + 1) * height]
                for k in range(2)
                for s in range(2)
                for _ in range(pairs)
            ],
            axis=0,
        )
        constant = pltpu.roll(dot_rows(repeated, lefts), 2 * band_rows, 1)
        first = split(lefts)
        kept_swap.wait_recv()
        kept_half = split(kept_in[...].reshape(plane * height, half))

    with jax.named_scope("shares"):
        wait_for(shares.at[pl.ds(0, plane - 1)], share_got)
        quarters = []
        for q in range(4):
            total = shares[q * pairs]
            for i in range(1, pairs):
                total = total + shares[q * pairs + i]
            quarters.append(total)
        sum0 = jnp.concatenate(quarters[:2], axis=1)
        sum1 = jnp.concatenate(quarters[2:], axis=1)
        upper0 = -sum0 * flag0
        for h in range(2):
            gather_out[h, :, :width] = upper0
            gather_out[h, :, width:] = quarters[2 + h]
        gather_in[slot_me] = gather_out[side]

    with jax.named_scope("gather"):

        @each_chip
        def _(p, s, number):
            pltpu.make_async_remote_copy(
                src_ref=gather_out.at[s],
                dst_ref=gather_in.at[slot_me],
                send_sem=gather_sent,
                recv_sem=gather_got.at[number],
                device_id=(2 * p + core, 2 * z + s),
                device_id_type=MESH,
            ).start()

        chip_copy(gather_in.at[slot_me], gather_in.at[slot_me], pass_sent, pass_got).start()
        upper_ref[0] = upper0
        upper_ref[1] = -(sum1 + dot(upper0, link_ref[...])) * flag1

        def forward(p, s, number):
            arrived = gather_in.at[(core * 2 + s) * pairs + p]
            wait_for(arrived, gather_got.at[number])
            chip_copy(arrived, arrived, pass_sent, pass_got).start()

        forward(pair, 1 - side, 1)

        @pl.loop(1, pairs)
        def _(step):
            other = wrap(pair + pairs - step, pairs)
            forward(other, side, 2 * step)
            forward(other, 1 - side, 2 * step + 1)

        wait_for(gather_in.at[mine], pass_got)

    with jax.named_scope("diagonal"):
        uppers = split(gather_in[:, :, :width].reshape(plane * height, width))
        sums = split(gather_in[:, :, width:].reshape(plane * height, half))
        chained_half = split(dot_split(uppers, link_half))
        chained_group = split(dot_split(uppers, link_group))
        upper_half = split(gather_in[:, :, column_half].reshape(plane * height, half))
        turn = lax.rem(LANES + band_rows - lax.rem(row, per) * band_rows, LANES)
        later = (
            dot_split(sums, first, 0)
            + pltpu.roll(dot_split(chained_half, first, 0), LANES - band_rows, 1)
            + pltpu.roll(dot_split(kept_half, chained_group, 0), turn, 1)
            + constant
        )
        lane = lax.broadcasted_iota(jnp.int32, (half, LANES), 1)
        tiles = jnp.where(lane < band_rows, -dot_split(upper_half, first, 0), later)
        low = lane[:8] < 2 * band_rows
        for j in range(count):
            top = tiles[band_cols * j : band_cols * j + 8]
            bottom = tiles[band_cols * j + 8 : band_cols * j + 16]
            tile_out[j] = jnp.where(low, top, pltpu.roll(bottom, 2 * band_rows, 1))

    with jax.named_scope("tiles"):

        for other in range(count):
            target = side * count + other

            def send():
                pltpu.make_async_remote_copy(
                    src_ref=tile_out.at[other],
                    dst_ref=tile_in.at[z],
                    send_sem=tile_sent,
                    recv_sem=tile_got,
                    device_id=(row, target),
                    device_id_type=MESH,
                ).start()

            pl.when(target != col)(send)

            @pl.when(target == col)
            def _():
                pltpu.make_async_copy(tile_out.at[other], tile_in.at[z], tile_got).start()

        wait_for(tile_in, tile_got)
        total = tile_in[0]
        for i in range(1, depth):
            total = total + tile_in[i]
        for i in range(2):
            for s in range(2):
                at = (2 * i + s) * band_rows
                out_ref[s, 8 * i : 8 * i + 8, :] = diag_ref[s, 8 * i : 8 * i + 8, :] + total[:, at : at + band_rows]

    with jax.named_scope("drain"):
        for i in (1, 2, 3):
            anc_copy(i).wait_send()
        for j in (1, 2):
            far_copy(j).wait_send()
        extra_swap.wait_send()
        kept_swap.wait_send()

        @pl.when(own_slab)
        def _():
            wait_for(slab.at[pl.ds(0, 4 * rows - 1)], slab_sent)

        @pl.when(jnp.logical_not(own_slab))
        def _():
            wait_for(slab, slab_sent)

        wait_for(left_in.at[pl.ds(0, plane - 1)], left_sent)
        wait_for(kept_in.at[pl.ds(0, rows - 1)], kept_sent)
        wait_for(shares.at[pl.ds(0, plane - 1)], share_sent)
        wait_for(gather_in.at[pl.ds(0, rows - 1)], gather_sent)
        wait_for(gather_in.at[mine], pass_sent)

        @pl.when(own)
        def _():
            wait_for(tile_in.at[pl.ds(0, count - 1)], tile_sent)

        @pl.when(jnp.logical_not(own))
        def _():
            wait_for(tile_in, tile_sent)


def local(rows, cols, ancestor_inverse, pattern, listed, panels, parent_panels, diag_inverse):
    supers, height, width = panels.shape
    tall, wide = ancestor_inverse.shape
    depth = cols // 2
    plane = 2 * rows
    half = width // 2
    count = cols // 2
    vmem = pl.BlockSpec(memory_space=pltpu.VMEM)
    smem = pl.BlockSpec(memory_space=pltpu.SMEM)
    anywhere = pl.BlockSpec(memory_space=pl.ANY)
    turned = jnp.swapaxes(diag_inverse, 1, 2)
    upper, tiles = pl.pallas_call(
        functools.partial(kernel, rows, cols),
        out_shape=(
            jax.ShapeDtypeStruct(panels.shape, F32),
            jax.ShapeDtypeStruct(turned.shape, F32),
        ),
        in_specs=[anywhere, smem, smem, anywhere, anywhere, anywhere],
        out_specs=(vmem, vmem),
        scratch_shapes=[
            pltpu.VMEM(ancestor_inverse.shape, F32),
            pltpu.VMEM(panels.shape, F32),
            pltpu.VMEM((width, width), F32),
            pltpu.VMEM(turned.shape, F32),
            pltpu.VMEM((3, supers, height, width), F32),
            pltpu.VMEM((2, 2 * tall, wide), F32),
            pltpu.VMEM((4 * rows, height, half), F32),
            pltpu.VMEM((plane, height, half), F32),
            pltpu.VMEM((plane, height, half), F32),
            pltpu.VMEM((rows, height, LANES), F32),
            pltpu.VMEM((plane, height, LANES), F32),
            pltpu.VMEM((2, height, half), F32),
            pltpu.VMEM((plane, height, half), F32),
            pltpu.VMEM((2, height, width + half), F32),
            pltpu.VMEM((plane, height, width + half), F32),
            pltpu.VMEM((count, 8, LANES), F32),
            pltpu.VMEM((depth, 8, LANES), F32),
            pltpu.VMEM((2, height, width), F32),
            pltpu.VMEM((height, width), F32),
            pltpu.SemaphoreType.DMA((4,)),
            pltpu.SemaphoreType.DMA((3,)),
            pltpu.SemaphoreType.DMA((3,)),
            pltpu.SemaphoreType.DMA((2,)),
            pltpu.SemaphoreType.DMA((2,)),
            pltpu.SemaphoreType.DMA((rows,)),
            pltpu.SemaphoreType.REGULAR,
            pltpu.SemaphoreType.DMA((17,)),
        ],
        compiler_params=pltpu.CompilerParams(
            collective_id=0, has_side_effects=True, vmem_limit_bytes=56 * 1024 * 1024
        ),
    )(ancestor_inverse, pattern, listed, panels, parent_panels[0], turned)
    return upper, jnp.swapaxes(tiles, 1, 2)


def solution(mesh):
    rows, cols = mesh.shape["row"], mesh.shape["col"]
    return jax.shard_map(
        functools.partial(local, rows, cols),
        mesh=mesh,
        in_specs=(
            P("row", "col"),
            P(),
            P(),
            P(None, ("col", "row"), None),
            P(),
            P(None, "row", "col"),
        ),
        out_specs=(P(None, ("col", "row"), None), P(None, "row", "col")),
        check_vma=False,
    )
```

```python
import functools

import jax
import jax.numpy as jnp
from jax import lax
from jax.experimental import pallas as pl
from jax.experimental.pallas import tpu as pltpu
from jax.sharding import PartitionSpec as P

BLK = 128
LANES = 128
STRIDE = 5
HOPS = (3, 2, -2, 1, -1)
MESH = pl.DeviceIdType.MESH
F32 = jnp.float32


def dot(left, right):
    return jnp.dot(left, right, precision=lax.Precision.HIGHEST, preferred_element_type=F32)


def dot_rows(left, right):
    return lax.dot_general(
        left,
        right,
        (((0,), (0,)), ((), ())),
        precision=lax.Precision.HIGHEST,
        preferred_element_type=F32,
    )


def split(value):
    high = value.astype(jnp.bfloat16)
    return high, (value - high.astype(F32)).astype(jnp.bfloat16)


def dot_split(left, right, dim=1):
    def once(a, b):
        return lax.dot_general(a, b, (((dim,), (0,)), ((), ())), preferred_element_type=F32)

    return once(left[0], right[1]) + once(left[1], right[0]) + once(left[0], right[0])


def exchange(parts, width):
    parts = list(parts)
    count = len(parts)
    segment = lax.broadcasted_iota(jnp.int32, parts[0].shape, 1) // width
    bit = count // 2
    while bit:
        low = (segment % (2 * bit)) < bit
        for a in range(count):
            if a & bit == 0:
                first, second = parts[a], parts[a + bit]
                parts[a] = jnp.where(low, first, pltpu.roll(second, bit * width, 1))
                parts[a + bit] = jnp.where(low, pltpu.roll(first, LANES - bit * width, 1), second)
        bit //= 2
    return parts


def kernel(
    rows,
    cols,
    a_hbm,
    pattern_ref,
    listed_ref,
    panel_hbm,
    link_hbm,
    diag_hbm,
    upper_ref,
    out_ref,
    a_ref,
    panel_ref,
    link_ref,
    diag_ref,
    panels,
    anc,
    slab,
    partial,
    shares,
    left_out,
    left_in,
    kept_out,
    kept_in,
    gather_out,
    gather_in,
    tile_out,
    tile_in,
    extra_out,
    extra_in,
    load_sems,
    anc_send,
    anc_recv,
    far_send,
    far_recv,
    gather_got,
    ready,
    sems,
):
    row, col = lax.axis_index("row"), lax.axis_index("col")
    depth = cols // 2
    z, side = lax.div(col, 2), lax.rem(col, 2)
    pair, core = lax.div(row, 2), lax.rem(row, 2)
    pairs = rows // 2
    height = panel_ref.shape[1]
    width = panel_ref.shape[2]
    half = width // 2
    plane = 2 * rows
    me = side * rows + row
    slot_me = (core * 2 + side) * pairs + pair
    tall = a_ref.shape[0]
    band_rows = width // rows
    band_cols = width // cols
    count = cols // 2
    own = lax.div(col, count) == side

    (slab_sent, slab_got, left_sent, left_got, kept_sent, kept_got, share_sent, share_got) = (
        sems.at[i] for i in range(8)
    )
    gather_sent, pass_sent, pass_got, tile_sent, tile_got = (sems.at[i] for i in range(8, 13))
    extra_sent, extra_got, forward_sent, forward_got = (sems.at[i] for i in range(13, 17))

    def wait_for(ref, sem):
        pltpu.make_async_copy(ref, ref, sem).wait()

    def wrap(value, size):
        return jnp.where(value >= size, value - size, value)

    def plane_at(offset):
        return wrap(z + offset % depth, depth)

    def each_peer(act):
        act(row, 1 - side)

        @pl.loop(1, rows)
        def _(step):
            other = wrap(row + step, rows)
            act(other, side)
            act(other, 1 - side)

    def each_chip(act):
        act(pair, 1 - side, 1)

        @pl.loop(1, pairs)
        def _(step):
            other = wrap(pair + step, pairs)
            act(other, side, 2 * step)
            act(other, 1 - side, 2 * step + 1)

    held = [(0, (*HOPS[1:], 0)), (-STRIDE, (*HOPS, 0)), (STRIDE, (*HOPS[1:], 0))]
    own_slab = functools.reduce(jnp.logical_or, [lax.div(plane_at(offset), 2) == pair for offset, _ in held])

    loads = [
        pltpu.make_async_copy(panel_hbm, panel_ref, load_sems.at[0]),
        pltpu.make_async_copy(a_hbm, a_ref, load_sems.at[1]),
        pltpu.make_async_copy(diag_hbm, diag_ref, load_sems.at[2]),
        pltpu.make_async_copy(link_hbm, link_ref, load_sems.at[3]),
    ]
    with jax.named_scope("greet"):
        for load in loads:
            load.start()
        barrier = pltpu.get_barrier_semaphore()

        def greet(device):
            pl.semaphore_signal(barrier, inc=1, device_id=device, device_id_type=MESH)

        for offset in (*HOPS, STRIDE, -STRIDE):
            greet((row, 2 * plane_at(offset) + side))
        each_peer(lambda r, s: greet((r, 2 * z + s)))

        def keep(s):
            found = listed_ref[s, 0] == col
            for i in range(1, listed_ref.shape[1]):
                found = jnp.logical_or(found, listed_ref[s, i] == col)
            return jnp.where(found, 1.0, 0.0).astype(F32)

        flag0, flag1 = keep(0), keep(1)
        loads[0].wait()
        kept0 = panel_ref[0] * flag0
        kept1 = panel_ref[1] * flag1
        panels[0, 0] = kept0
        panels[0, 1] = kept1
        loads[1].wait()
        for i in range(tall // BLK):
            present = pattern_ref[(tall // BLK) * row + i, col].astype(F32)
            anc[side, pl.ds(core * tall + i * BLK, BLK), :] = a_ref[pl.ds(i * BLK, BLK), :] * present
        pl.semaphore_wait(barrier, plane - 1 + len(HOPS) + 2)

    def far_copy(j):
        return pltpu.make_async_remote_copy(
            src_ref=panels.at[0],
            dst_ref=panels.at[j],
            send_sem=far_send.at[j - 1],
            recv_sem=far_recv.at[j - 1],
            device_id=(row, 2 * plane_at(STRIDE if j == 1 else -STRIDE) + side),
            device_id_type=MESH,
        )

    def spread(j):
        back, offsets = held[j]
        block = plane_at(back)
        owner = lax.div(block, 2)
        slot = (lax.rem(block, 2) * 2 + side) * rows + row
        for offset in offsets:
            for step in range(4):
                super_of = core if step < 2 else 1 - core
                half_of = side if step % 2 == 0 else 1 - side
                source = panels.at[j, super_of, :, pl.ds(pl.multiple_of(half_of * half, LANES), half)]

                def send():
                    pltpu.make_async_remote_copy(
                        src_ref=source,
                        dst_ref=slab.at[slot],
                        send_sem=slab_sent,
                        recv_sem=slab_got,
                        device_id=(2 * owner + super_of, 2 * plane_at(offset) + half_of),
                        device_id_type=MESH,
                    ).start()

                if step == 0 and offset == 0:
                    pl.when(owner != pair)(send)

                    @pl.when(owner == pair)
                    def _():
                        pltpu.make_async_copy(source, slab.at[slot], slab_got).start()
                else:
                    send()

    def anc_copy(i):
        piece = anc.at[1 - side if i == 3 else side, pl.ds(core * tall, tall), :]
        return pltpu.make_async_remote_copy(
            src_ref=piece,
            dst_ref=piece,
            send_sem=anc_send.at[i - 1],
            recv_sem=anc_recv.at[i - 1],
            device_id=(row, 2 * z + 1 - side) if i == 2 else (2 * pair + 1 - core, col),
            device_id_type=MESH,
        )

    def chip_copy(source, target, sent, got):
        return pltpu.make_async_remote_copy(
            src_ref=source,
            dst_ref=target,
            send_sem=sent,
            recv_sem=got,
            device_id=(2 * pair + 1 - core, col),
            device_id_type=MESH,
        )

    with jax.named_scope("start"):
        for j in (1, 2):
            far_copy(j).start()
        for offset in HOPS:
            pl.semaphore_signal(
                ready, inc=1, device_id=(row, 2 * plane_at(-offset) + side), device_id_type=MESH
            )
        for i in (2, 1):
            anc_copy(i).start()

    with jax.named_scope("early"):
        for h in range(2):
            kept_out[h] = kept1[:, h * half : (h + 1) * half]
        kept_in[slot_me] = kept_out[side]

        def send_kept(p, s, _):
            pltpu.make_async_remote_copy(
                src_ref=kept_out.at[s],
                dst_ref=kept_in.at[slot_me],
                send_sem=kept_sent,
                recv_sem=kept_got,
                device_id=(2 * p + core, 2 * z + s),
                device_id_type=MESH,
            ).start()

        loads[2].wait()
        loads[3].wait()
        mixed = kept1 - dot(kept0, link_ref[...])
        link_band = link_ref[pl.ds(pl.multiple_of(row * band_rows, 8), band_rows), :]
        extra = dot(diag_ref[0], link_band)
        for h in range(2):
            extra_out[h] = extra[h * height : (h + 1) * height]
        extra_swap = chip_copy(extra_out.at[1 - core], extra_in, extra_sent, extra_got)
        extra_swap.start()
        pl.semaphore_wait(ready, len(HOPS))
        spread(0)
        each_chip(send_kept)
        extra_swap.wait_recv()
        extra = extra_out[core] + extra_in[...]
        per = LANES // band_rows
        for g in range(width // LANES):
            cut = slice(g * LANES, (g + 1) * LANES)
            packed = exchange([kept0[:, cut], kept1[:, cut], mixed[:, cut], extra[:, cut]], band_rows)
            for j in range(per):
                left_out[g * per + j] = packed[j]
        left_in[slot_me] = left_out[row]

        @each_peer
        def _(r, s):
            pltpu.make_async_remote_copy(
                src_ref=left_out.at[r],
                dst_ref=left_in.at[slot_me],
                send_sem=left_sent,
                recv_sem=left_got,
                device_id=(r, 2 * z + s),
                device_id_type=MESH,
            ).start()

    with jax.named_scope("spread"):
        for j in (1, 2):
            far_copy(j).wait_recv()
            spread(j)
        anc_copy(2).wait_recv()
        anc_copy(3).start()

    with jax.named_scope("slab"):
        for i in (1, 3):
            anc_copy(i).wait_recv()
        wait_for(slab, slab_got)
    with jax.named_scope("product"):
        kept_rows = split(slab[...].reshape(2 * tall, half))
        for i in range(2):
            part = dot_split(split(anc[i]), kept_rows, 0)
            partial[pl.ds(i * rows, rows)] = part.reshape(rows, height, half)

    slot = (2 * core + side) * pairs + pair
    with jax.named_scope("scatter"):
        shares[slot] = partial[me]

        @each_peer
        def _(r, s):
            pltpu.make_async_remote_copy(
                src_ref=partial.at[s * rows + r],
                dst_ref=shares.at[slot],
                send_sem=share_sent,
                recv_sem=share_got,
                device_id=(r, 2 * z + s),
                device_id_type=MESH,
            ).start()

    with jax.named_scope("linkterm"):
        wait_for(kept_in.at[pl.ds(0, rows - 1)], kept_got)
        mine = pl.ds(core * rows, rows)
        kept_swap = chip_copy(kept_in.at[mine], kept_in.at[mine], forward_sent, forward_got)
        kept_swap.start()
        wait_for(left_in.at[pl.ds(0, plane - 1)], left_got)
        lefts = left_in[...].reshape(plane * height, LANES)
        column_half = pl.ds(pl.multiple_of(side * half, LANES), half)
        group = pl.ds(pl.multiple_of(lax.div(row, per) * LANES, LANES), LANES)
        link_half = split(link_ref[:, column_half])
        link_group = split(link_ref[:, group])
        link_rows = link_ref[pl.ds(pl.multiple_of(z * 2 * band_cols, 8), 2 * band_cols), column_half]
        repeated = jnp.concatenate(
            [
                link_rows[s * band_cols + k * height : s * band_cols + (k + 1) * height]
                for k in range(2)
                for s in range(2)
                for _ in range(pairs)
            ],
            axis=0,
        )
        constant = pltpu.roll(dot_rows(repeated, lefts), 2 * band_rows, 1)
        first = split(lefts)
        kept_swap.wait_recv()
        kept_half = split(kept_in[...].reshape(plane * height, half))

    with jax.named_scope("shares"):
        wait_for(shares.at[pl.ds(0, plane - 1)], share_got)
        quarters = []
        for q in range(4):
            total = shares[q * pairs]
            for i in range(1, pairs):
                total = total + shares[q * pairs + i]
            quarters.append(total)
        sum0 = jnp.concatenate(quarters[:2], axis=1)
        sum1 = jnp.concatenate(quarters[2:], axis=1)
        upper0 = -sum0 * flag0
        for h in range(2):
            gather_out[h, :, :width] = upper0
            gather_out[h, :, width:] = quarters[2 + h]
        gather_in[slot_me] = gather_out[side]

    with jax.named_scope("gather"):

        @each_chip
        def _(p, s, number):
            pltpu.make_async_remote_copy(
                src_ref=gather_out.at[s],
                dst_ref=gather_in.at[slot_me],
                send_sem=gather_sent,
                recv_sem=gather_got.at[number],
                device_id=(2 * p + core, 2 * z + s),
                device_id_type=MESH,
            ).start()

        chip_copy(gather_in.at[slot_me], gather_in.at[slot_me], pass_sent, pass_got).start()
        upper_ref[0] = upper0
        upper_ref[1] = -(sum1 + dot(upper0, link_ref[...])) * flag1

        def forward(p, s, number):
            arrived = gather_in.at[(core * 2 + s) * pairs + p]
            wait_for(arrived, gather_got.at[number])
            chip_copy(arrived, arrived, pass_sent, pass_got).start()

        forward(pair, 1 - side, 1)

        @pl.loop(1, pairs)
        def _(step):
            other = wrap(pair + pairs - step, pairs)
            forward(other, side, 2 * step)
            forward(other, 1 - side, 2 * step + 1)

        wait_for(gather_in.at[mine], pass_got)

    with jax.named_scope("diagonal"):
        uppers = split(gather_in[:, :, :width].reshape(plane * height, width))
        sums = split(gather_in[:, :, width:].reshape(plane * height, half))
        chained_half = split(dot_split(uppers, link_half))
        chained_group = split(dot_split(uppers, link_group))
        upper_half = split(gather_in[:, :, column_half].reshape(plane * height, half))
        turn = lax.rem(LANES + band_rows - lax.rem(row, per) * band_rows, LANES)
        later = (
            dot_split(sums, first, 0)
            + pltpu.roll(dot_split(chained_half, first, 0), LANES - band_rows, 1)
            + pltpu.roll(dot_split(kept_half, chained_group, 0), turn, 1)
            + constant
        )
        lane = lax.broadcasted_iota(jnp.int32, (half, LANES), 1)
        tiles = jnp.where(lane < band_rows, -dot_split(upper_half, first, 0), later)
        low = lane[:8] < 2 * band_rows
        for j in range(count):
            top = tiles[band_cols * j : band_cols * j + 8]
            bottom = tiles[band_cols * j + 8 : band_cols * j + 16]
            tile_out[j] = jnp.where(low, top, pltpu.roll(bottom, 2 * band_rows, 1))

    with jax.named_scope("tiles"):

        for other in range(count):
            target = side * count + other

            def send():
                pltpu.make_async_remote_copy(
                    src_ref=tile_out.at[other],
                    dst_ref=tile_in.at[z],
                    send_sem=tile_sent,
                    recv_sem=tile_got,
                    device_id=(row, target),
                    device_id_type=MESH,
                ).start()

            pl.when(target != col)(send)

            @pl.when(target == col)
            def _():
                pltpu.make_async_copy(tile_out.at[other], tile_in.at[z], tile_got).start()

        wait_for(tile_in, tile_got)
        total = tile_in[0]
        for i in range(1, depth):
            total = total + tile_in[i]
        for i in range(2):
            for s in range(2):
                at = (2 * i + s) * band_rows
                out_ref[s, 8 * i : 8 * i + 8, :] = diag_ref[s, 8 * i : 8 * i + 8, :] + total[:, at : at + band_rows]

    with jax.named_scope("drain"):
        for i in (1, 2, 3):
            anc_copy(i).wait_send()
        for j in (1, 2):
            far_copy(j).wait_send()
        extra_swap.wait_send()
        kept_swap.wait_send()

        @pl.when(own_slab)
        def _():
            wait_for(slab.at[pl.ds(0, 4 * rows - 1)], slab_sent)

        @pl.when(jnp.logical_not(own_slab))
        def _():
            wait_for(slab, slab_sent)

        wait_for(left_in.at[pl.ds(0, plane - 1)], left_sent)
        wait_for(kept_in.at[pl.ds(0, rows - 1)], kept_sent)
        wait_for(shares.at[pl.ds(0, plane - 1)], share_sent)
        wait_for(gather_in.at[pl.ds(0, rows - 1)], gather_sent)
        wait_for(gather_in.at[mine], pass_sent)

        @pl.when(own)
        def _():
            wait_for(tile_in.at[pl.ds(0, count - 1)], tile_sent)

        @pl.when(jnp.logical_not(own))
        def _():
            wait_for(tile_in, tile_sent)


def local(rows, cols, ancestor_inverse, pattern, listed, panels, parent_panels, diag_inverse):
    supers, height, width = panels.shape
    tall, wide = ancestor_inverse.shape
    depth = cols // 2
    plane = 2 * rows
    half = width // 2
    count = cols // 2
    vmem = pl.BlockSpec(memory_space=pltpu.VMEM)
    smem = pl.BlockSpec(memory_space=pltpu.SMEM)
    anywhere = pl.BlockSpec(memory_space=pl.ANY)
    turned = jnp.swapaxes(diag_inverse, 1, 2)
    upper, tiles = pl.pallas_call(
        functools.partial(kernel, rows, cols),
        out_shape=(
            jax.ShapeDtypeStruct(panels.shape, F32),
            jax.ShapeDtypeStruct(turned.shape, F32),
        ),
        in_specs=[anywhere, smem, smem, anywhere, anywhere, anywhere],
        out_specs=(vmem, vmem),
        scratch_shapes=[
            pltpu.VMEM(ancestor_inverse.shape, F32),
            pltpu.VMEM(panels.shape, F32),
            pltpu.VMEM((width, width), F32),
            pltpu.VMEM(turned.shape, F32),
            pltpu.VMEM((3, supers, height, width), F32),
            pltpu.VMEM((2, 2 * tall, wide), F32),
            pltpu.VMEM((4 * rows, height, half), F32),
            pltpu.VMEM((plane, height, half), F32),
            pltpu.VMEM((plane, height, half), F32),
            pltpu.VMEM((rows, height, LANES), F32),
            pltpu.VMEM((plane, height, LANES), F32),
            pltpu.VMEM((2, height, half), F32),
            pltpu.VMEM((plane, height, half), F32),
            pltpu.VMEM((2, height, width + half), F32),
            pltpu.VMEM((plane, height, width + half), F32),
            pltpu.VMEM((count, 8, LANES), F32),
            pltpu.VMEM((depth, 8, LANES), F32),
            pltpu.VMEM((2, height, width), F32),
            pltpu.VMEM((height, width), F32),
            pltpu.SemaphoreType.DMA((4,)),
            pltpu.SemaphoreType.DMA((3,)),
            pltpu.SemaphoreType.DMA((3,)),
            pltpu.SemaphoreType.DMA((2,)),
            pltpu.SemaphoreType.DMA((2,)),
            pltpu.SemaphoreType.DMA((rows,)),
            pltpu.SemaphoreType.REGULAR,
            pltpu.SemaphoreType.DMA((17,)),
        ],
        compiler_params=pltpu.CompilerParams(
            collective_id=0, has_side_effects=True, vmem_limit_bytes=56 * 1024 * 1024
        ),
    )(ancestor_inverse, pattern, listed, panels, parent_panels[0], turned)
    return upper, jnp.swapaxes(tiles, 1, 2)


def solution(mesh):
    rows, cols = mesh.shape["row"], mesh.shape["col"]
    return jax.shard_map(
        functools.partial(local, rows, cols),
        mesh=mesh,
        in_specs=(
            P("row", "col"),
            P(),
            P(),
            P(None, ("col", "row"), None),
            P(),
            P(None, "row", "col"),
        ),
        out_specs=(P(None, ("col", "row"), None), P(None, "row", "col")),
        check_vma=False,
    )
```

```python
import functools

import jax
import jax.numpy as jnp
from jax import lax
from jax.experimental import pallas as pl
from jax.experimental.pallas import tpu as pltpu
from jax.sharding import PartitionSpec as P

BLK = 128
LANES = 128
STRIDE = 5
HOPS = (3, 2, -2, 1, -1)
MESH = pl.DeviceIdType.MESH
F32 = jnp.float32


def dot(left, right):
    return jnp.dot(left, right, precision=lax.Precision.HIGHEST, preferred_element_type=F32)


def dot_rows(left, right):
    return lax.dot_general(
        left,
        right,
        (((0,), (0,)), ((), ())),
        precision=lax.Precision.HIGHEST,
        preferred_element_type=F32,
    )


def split(value):
    high = value.astype(jnp.bfloat16)
    return high, (value - high.astype(F32)).astype(jnp.bfloat16)


def dot_split(left, right, dim=1):
    def once(a, b):
        return lax.dot_general(a, b, (((dim,), (0,)), ((), ())), preferred_element_type=F32)

    return once(left[0], right[1]) + once(left[1], right[0]) + once(left[0], right[0])


def exchange(parts, width):
    parts = list(parts)
    count = len(parts)
    segment = lax.broadcasted_iota(jnp.int32, parts[0].shape, 1) // width
    bit = count // 2
    while bit:
        low = (segment % (2 * bit)) < bit
        for a in range(count):
            if a & bit == 0:
                first, second = parts[a], parts[a + bit]
                parts[a] = jnp.where(low, first, pltpu.roll(second, bit * width, 1))
                parts[a + bit] = jnp.where(low, pltpu.roll(first, LANES - bit * width, 1), second)
        bit //= 2
    return parts


def kernel(
    rows,
    cols,
    a_hbm,
    pattern_ref,
    listed_ref,
    panel_hbm,
    link_hbm,
    diag_hbm,
    upper_ref,
    out_ref,
    a_ref,
    panel_ref,
    link_ref,
    diag_ref,
    panels,
    anc,
    slab,
    partial,
    shares,
    left_out,
    left_in,
    kept_out,
    kept_in,
    gather_out,
    gather_in,
    tile_out,
    tile_in,
    extra_out,
    extra_in,
    load_sems,
    anc_send,
    anc_recv,
    far_send,
    far_recv,
    gather_got,
    ready,
    sems,
):
    row, col = lax.axis_index("row"), lax.axis_index("col")
    depth = cols // 2
    z, side = lax.div(col, 2), lax.rem(col, 2)
    pair, core = lax.div(row, 2), lax.rem(row, 2)
    pairs = rows // 2
    height = panel_ref.shape[1]
    width = panel_ref.shape[2]
    half = width // 2
    plane = 2 * rows
    me = side * rows + row
    slot_me = (core * 2 + side) * pairs + pair
    tall = a_ref.shape[0]
    band_rows = width // rows
    band_cols = width // cols
    count = cols // 2
    own = lax.div(col, count) == side

    (slab_sent, slab_got, left_sent, left_got, kept_sent, kept_got, share_sent, share_got) = (
        sems.at[i] for i in range(8)
    )
    gather_sent, pass_sent, pass_got, tile_sent, tile_got = (sems.at[i] for i in range(8, 13))
    extra_sent, extra_got, forward_sent, forward_got = (sems.at[i] for i in range(13, 17))

    def wait_for(ref, sem):
        pltpu.make_async_copy(ref, ref, sem).wait()

    def wrap(value, size):
        return jnp.where(value >= size, value - size, value)

    def plane_at(offset):
        return wrap(z + offset % depth, depth)

    def each_peer(act):
        act(row, 1 - side)

        @pl.loop(1, rows)
        def _(step):
            other = wrap(row + step, rows)
            act(other, side)
            act(other, 1 - side)

    def each_chip(act):
        act(pair, 1 - side, 1)

        @pl.loop(1, pairs)
        def _(step):
            other = wrap(pair + step, pairs)
            act(other, side, 2 * step)
            act(other, 1 - side, 2 * step + 1)

    held = [(0, (*HOPS[1:], 0)), (-STRIDE, (*HOPS, 0)), (STRIDE, (*HOPS[1:], 0))]
    own_slab = functools.reduce(jnp.logical_or, [lax.div(plane_at(offset), 2) == pair for offset, _ in held])

    loads = [
        pltpu.make_async_copy(panel_hbm, panel_ref, load_sems.at[0]),
        pltpu.make_async_copy(a_hbm, a_ref, load_sems.at[1]),
        pltpu.make_async_copy(diag_hbm, diag_ref, load_sems.at[2]),
        pltpu.make_async_copy(link_hbm, link_ref, load_sems.at[3]),
    ]
    with jax.named_scope("greet"):
        for load in loads:
            load.start()
        barrier = pltpu.get_barrier_semaphore()

        def greet(device):
            pl.semaphore_signal(barrier, inc=1, device_id=device, device_id_type=MESH)

        for offset in (*HOPS, STRIDE, -STRIDE):
            greet((row, 2 * plane_at(offset) + side))
        each_peer(lambda r, s: greet((r, 2 * z + s)))

        def keep(s):
            found = listed_ref[s, 0] == col
            for i in range(1, listed_ref.shape[1]):
                found = jnp.logical_or(found, listed_ref[s, i] == col)
            return jnp.where(found, 1.0, 0.0).astype(F32)

        flag0, flag1 = keep(0), keep(1)
        loads[0].wait()
        kept0 = panel_ref[0] * flag0
        kept1 = panel_ref[1] * flag1
        panels[0, 0] = kept0
        panels[0, 1] = kept1
        loads[1].wait()
        for i in range(tall // BLK):
            present = pattern_ref[(tall // BLK) * row + i, col].astype(F32)
            anc[side, pl.ds(core * tall + i * BLK, BLK), :] = a_ref[pl.ds(i * BLK, BLK), :] * present
        pl.semaphore_wait(barrier, plane - 1 + len(HOPS) + 2)

    def far_copy(j, super_of):
        return pltpu.make_async_remote_copy(
            src_ref=panels.at[0, super_of],
            dst_ref=panels.at[j, super_of],
            send_sem=far_send.at[j - 1, super_of],
            recv_sem=far_recv.at[j - 1, super_of],
            device_id=(row, 2 * plane_at(STRIDE if j == 1 else -STRIDE) + side),
            device_id_type=MESH,
        )

    def spread(j, super_of):
        back, offsets = held[j]
        block = plane_at(back)
        owner = lax.div(block, 2)
        slot = (lax.rem(block, 2) * 2 + side) * rows + row
        for offset in offsets:
            for step in range(2):
                half_of = side if step == 0 else 1 - side
                source = panels.at[j, super_of, :, pl.ds(pl.multiple_of(half_of * half, LANES), half)]

                def send():
                    pltpu.make_async_remote_copy(
                        src_ref=source,
                        dst_ref=slab.at[slot],
                        send_sem=slab_sent,
                        recv_sem=slab_got,
                        device_id=(2 * owner + super_of, 2 * plane_at(offset) + half_of),
                        device_id_type=MESH,
                    ).start()

                if step == 0 and offset == 0:
                    here = jnp.logical_and(owner == pair, core == super_of)
                    pl.when(jnp.logical_not(here))(send)

                    @pl.when(here)
                    def _():
                        pltpu.make_async_copy(source, slab.at[slot], slab_got).start()
                else:
                    send()

    def anc_copy(i):
        piece = anc.at[1 - side if i == 3 else side, pl.ds(core * tall, tall), :]
        return pltpu.make_async_remote_copy(
            src_ref=piece,
            dst_ref=piece,
            send_sem=anc_send.at[i - 1],
            recv_sem=anc_recv.at[i - 1],
            device_id=(row, 2 * z + 1 - side) if i == 2 else (2 * pair + 1 - core, col),
            device_id_type=MESH,
        )

    def chip_copy(source, target, sent, got):
        return pltpu.make_async_remote_copy(
            src_ref=source,
            dst_ref=target,
            send_sem=sent,
            recv_sem=got,
            device_id=(2 * pair + 1 - core, col),
            device_id_type=MESH,
        )

    with jax.named_scope("start"):
        for super_of in range(2):
            for j in (1, 2):
                far_copy(j, super_of).start()
        for offset in HOPS:
            pl.semaphore_signal(
                ready, inc=1, device_id=(row, 2 * plane_at(-offset) + side), device_id_type=MESH
            )
        for i in (2, 1):
            anc_copy(i).start()

    with jax.named_scope("early"):
        for h in range(2):
            kept_out[h] = kept1[:, h * half : (h + 1) * half]
        kept_in[slot_me] = kept_out[side]

        def send_kept(p, s, _):
            pltpu.make_async_remote_copy(
                src_ref=kept_out.at[s],
                dst_ref=kept_in.at[slot_me],
                send_sem=kept_sent,
                recv_sem=kept_got,
                device_id=(2 * p + core, 2 * z + s),
                device_id_type=MESH,
            ).start()

        loads[2].wait()
        loads[3].wait()
        mixed = kept1 - dot(kept0, link_ref[...])
        link_band = link_ref[pl.ds(pl.multiple_of(row * band_rows, 8), band_rows), :]
        extra = dot(diag_ref[0], link_band)
        for h in range(2):
            extra_out[h] = extra[h * height : (h + 1) * height]
        extra_swap = chip_copy(extra_out.at[1 - core], extra_in, extra_sent, extra_got)
        extra_swap.start()
        pl.semaphore_wait(ready, len(HOPS))
        for super_of in range(2):
            spread(0, super_of)
        each_chip(send_kept)
        extra_swap.wait_recv()
        extra = extra_out[core] + extra_in[...]
        per = LANES // band_rows
        for g in range(width // LANES):
            cut = slice(g * LANES, (g + 1) * LANES)
            packed = exchange([kept0[:, cut], kept1[:, cut], mixed[:, cut], extra[:, cut]], band_rows)
            for j in range(per):
                left_out[g * per + j] = packed[j]
        left_in[slot_me] = left_out[row]

        @each_peer
        def _(r, s):
            pltpu.make_async_remote_copy(
                src_ref=left_out.at[r],
                dst_ref=left_in.at[slot_me],
                send_sem=left_sent,
                recv_sem=left_got,
                device_id=(r, 2 * z + s),
                device_id_type=MESH,
            ).start()

    with jax.named_scope("spread"):
        for super_of in range(2):
            for j in (1, 2):
                far_copy(j, super_of).wait_recv()
                spread(j, super_of)
        anc_copy(2).wait_recv()
        anc_copy(3).start()

    with jax.named_scope("slab"):
        for i in (1, 3):
            anc_copy(i).wait_recv()
        wait_for(slab, slab_got)
    with jax.named_scope("product"):
        kept_rows = split(slab[...].reshape(2 * tall, half))
        for i in range(2):
            part = dot_split(split(anc[i]), kept_rows, 0)
            partial[pl.ds(i * rows, rows)] = part.reshape(rows, height, half)

    slot = (2 * core + side) * pairs + pair
    with jax.named_scope("scatter"):
        shares[slot] = partial[me]

        @each_peer
        def _(r, s):
            pltpu.make_async_remote_copy(
                src_ref=partial.at[s * rows + r],
                dst_ref=shares.at[slot],
                send_sem=share_sent,
                recv_sem=share_got,
                device_id=(r, 2 * z + s),
                device_id_type=MESH,
            ).start()

    with jax.named_scope("linkterm"):
        wait_for(kept_in.at[pl.ds(0, rows - 1)], kept_got)
        mine = pl.ds(core * rows, rows)
        kept_swap = chip_copy(kept_in.at[mine], kept_in.at[mine], forward_sent, forward_got)
        kept_swap.start()
        wait_for(left_in.at[pl.ds(0, plane - 1)], left_got)
        lefts = left_in[...].reshape(plane * height, LANES)
        column_half = pl.ds(pl.multiple_of(side * half, LANES), half)
        group = pl.ds(pl.multiple_of(lax.div(row, per) * LANES, LANES), LANES)
        link_half = split(link_ref[:, column_half])
        link_group = split(link_ref[:, group])
        link_rows = link_ref[pl.ds(pl.multiple_of(z * 2 * band_cols, 8), 2 * band_cols), column_half]
        repeated = jnp.concatenate(
            [
                link_rows[s * band_cols + k * height : s * band_cols + (k + 1) * height]
                for k in range(2)
                for s in range(2)
                for _ in range(pairs)
            ],
            axis=0,
        )
        constant = pltpu.roll(dot_rows(repeated, lefts), 2 * band_rows, 1)
        first = split(lefts)
        kept_swap.wait_recv()
        kept_half = split(kept_in[...].reshape(plane * height, half))

    with jax.named_scope("shares"):
        wait_for(shares.at[pl.ds(0, plane - 1)], share_got)
        quarters = []
        for q in range(4):
            total = shares[q * pairs]
            for i in range(1, pairs):
                total = total + shares[q * pairs + i]
            quarters.append(total)
        sum0 = jnp.concatenate(quarters[:2], axis=1)
        sum1 = jnp.concatenate(quarters[2:], axis=1)
        upper0 = -sum0 * flag0
        for h in range(2):
            gather_out[h, :, :width] = upper0
            gather_out[h, :, width:] = quarters[2 + h]
        gather_in[slot_me] = gather_out[side]

    with jax.named_scope("gather"):

        @each_chip
        def _(p, s, number):
            pltpu.make_async_remote_copy(
                src_ref=gather_out.at[s],
                dst_ref=gather_in.at[slot_me],
                send_sem=gather_sent,
                recv_sem=gather_got.at[number],
                device_id=(2 * p + core, 2 * z + s),
                device_id_type=MESH,
            ).start()

        chip_copy(gather_in.at[slot_me], gather_in.at[slot_me], pass_sent, pass_got).start()
        upper_ref[0] = upper0
        upper_ref[1] = -(sum1 + dot(upper0, link_ref[...])) * flag1

        def forward(p, s, number):
            arrived = gather_in.at[(core * 2 + s) * pairs + p]
            wait_for(arrived, gather_got.at[number])
            chip_copy(arrived, arrived, pass_sent, pass_got).start()

        forward(pair, 1 - side, 1)

        @pl.loop(1, pairs)
        def _(step):
            other = wrap(pair + pairs - step, pairs)
            forward(other, side, 2 * step)
            forward(other, 1 - side, 2 * step + 1)

        wait_for(gather_in.at[mine], pass_got)

    with jax.named_scope("diagonal"):
        uppers = split(gather_in[:, :, :width].reshape(plane * height, width))
        sums = split(gather_in[:, :, width:].reshape(plane * height, half))
        chained_half = split(dot_split(uppers, link_half))
        chained_group = split(dot_split(uppers, link_group))
        upper_half = split(gather_in[:, :, column_half].reshape(plane * height, half))
        turn = lax.rem(LANES + band_rows - lax.rem(row, per) * band_rows, LANES)
        later = (
            dot_split(sums, first, 0)
            + pltpu.roll(dot_split(chained_half, first, 0), LANES - band_rows, 1)
            + pltpu.roll(dot_split(kept_half, chained_group, 0), turn, 1)
            + constant
        )
        lane = lax.broadcasted_iota(jnp.int32, (half, LANES), 1)
        tiles = jnp.where(lane < band_rows, -dot_split(upper_half, first, 0), later)
        low = lane[:8] < 2 * band_rows
        for j in range(count):
            top = tiles[band_cols * j : band_cols * j + 8]
            bottom = tiles[band_cols * j + 8 : band_cols * j + 16]
            tile_out[j] = jnp.where(low, top, pltpu.roll(bottom, 2 * band_rows, 1))

    with jax.named_scope("tiles"):

        for other in range(count):
            target = side * count + other

            def send():
                pltpu.make_async_remote_copy(
                    src_ref=tile_out.at[other],
                    dst_ref=tile_in.at[z],
                    send_sem=tile_sent,
                    recv_sem=tile_got,
                    device_id=(row, target),
                    device_id_type=MESH,
                ).start()

            pl.when(target != col)(send)

            @pl.when(target == col)
            def _():
                pltpu.make_async_copy(tile_out.at[other], tile_in.at[z], tile_got).start()

        wait_for(tile_in, tile_got)
        total = tile_in[0]
        for i in range(1, depth):
            total = total + tile_in[i]
        for i in range(2):
            for s in range(2):
                at = (2 * i + s) * band_rows
                out_ref[s, 8 * i : 8 * i + 8, :] = diag_ref[s, 8 * i : 8 * i + 8, :] + total[:, at : at + band_rows]

    with jax.named_scope("drain"):
        for i in (1, 2, 3):
            anc_copy(i).wait_send()
        for super_of in range(2):
            for j in (1, 2):
                far_copy(j, super_of).wait_send()
        extra_swap.wait_send()
        kept_swap.wait_send()

        @pl.when(own_slab)
        def _():
            wait_for(slab.at[pl.ds(0, 4 * rows - 1)], slab_sent)

        @pl.when(jnp.logical_not(own_slab))
        def _():
            wait_for(slab, slab_sent)

        wait_for(left_in.at[pl.ds(0, plane - 1)], left_sent)
        wait_for(kept_in.at[pl.ds(0, rows - 1)], kept_sent)
        wait_for(shares.at[pl.ds(0, plane - 1)], share_sent)
        wait_for(gather_in.at[pl.ds(0, rows - 1)], gather_sent)
        wait_for(gather_in.at[mine], pass_sent)

        @pl.when(own)
        def _():
            wait_for(tile_in.at[pl.ds(0, count - 1)], tile_sent)

        @pl.when(jnp.logical_not(own))
        def _():
            wait_for(tile_in, tile_sent)


def local(rows, cols, ancestor_inverse, pattern, listed, panels, parent_panels, diag_inverse):
    supers, height, width = panels.shape
    tall, wide = ancestor_inverse.shape
    depth = cols // 2
    plane = 2 * rows
    half = width // 2
    count = cols // 2
    vmem = pl.BlockSpec(memory_space=pltpu.VMEM)
    smem = pl.BlockSpec(memory_space=pltpu.SMEM)
    anywhere = pl.BlockSpec(memory_space=pl.ANY)
    turned = jnp.swapaxes(diag_inverse, 1, 2)
    upper, tiles = pl.pallas_call(
        functools.partial(kernel, rows, cols),
        out_shape=(
            jax.ShapeDtypeStruct(panels.shape, F32),
            jax.ShapeDtypeStruct(turned.shape, F32),
        ),
        in_specs=[anywhere, smem, smem, anywhere, anywhere, anywhere],
        out_specs=(vmem, vmem),
        scratch_shapes=[
            pltpu.VMEM(ancestor_inverse.shape, F32),
            pltpu.VMEM(panels.shape, F32),
            pltpu.VMEM((width, width), F32),
            pltpu.VMEM(turned.shape, F32),
            pltpu.VMEM((3, supers, height, width), F32),
            pltpu.VMEM((2, 2 * tall, wide), F32),
            pltpu.VMEM((4 * rows, height, half), F32),
            pltpu.VMEM((plane, height, half), F32),
            pltpu.VMEM((plane, height, half), F32),
            pltpu.VMEM((rows, height, LANES), F32),
            pltpu.VMEM((plane, height, LANES), F32),
            pltpu.VMEM((2, height, half), F32),
            pltpu.VMEM((plane, height, half), F32),
            pltpu.VMEM((2, height, width + half), F32),
            pltpu.VMEM((plane, height, width + half), F32),
            pltpu.VMEM((count, 8, LANES), F32),
            pltpu.VMEM((depth, 8, LANES), F32),
            pltpu.VMEM((2, height, width), F32),
            pltpu.VMEM((height, width), F32),
            pltpu.SemaphoreType.DMA((4,)),
            pltpu.SemaphoreType.DMA((3,)),
            pltpu.SemaphoreType.DMA((3,)),
            pltpu.SemaphoreType.DMA((2, 2)),
            pltpu.SemaphoreType.DMA((2, 2)),
            pltpu.SemaphoreType.DMA((rows,)),
            pltpu.SemaphoreType.REGULAR,
            pltpu.SemaphoreType.DMA((17,)),
        ],
        compiler_params=pltpu.CompilerParams(
            collective_id=0, has_side_effects=True, vmem_limit_bytes=56 * 1024 * 1024
        ),
    )(ancestor_inverse, pattern, listed, panels, parent_panels[0], turned)
    return upper, jnp.swapaxes(tiles, 1, 2)


def solution(mesh):
    rows, cols = mesh.shape["row"], mesh.shape["col"]
    return jax.shard_map(
        functools.partial(local, rows, cols),
        mesh=mesh,
        in_specs=(
            P("row", "col"),
            P(),
            P(),
            P(None, ("col", "row"), None),
            P(),
            P(None, "row", "col"),
        ),
        out_specs=(P(None, ("col", "row"), None), P(None, "row", "col")),
        check_vma=False,
    )
```

```python
import functools

import jax
import jax.numpy as jnp
from jax import lax
from jax.experimental import pallas as pl
from jax.experimental.pallas import tpu as pltpu
from jax.sharding import PartitionSpec as P

BLK = 128
LANES = 128
STRIDE = 5
HOPS = (3, 2, -2, 1, -1)
MESH = pl.DeviceIdType.MESH
F32 = jnp.float32


def dot(left, right):
    return jnp.dot(left, right, precision=lax.Precision.HIGHEST, preferred_element_type=F32)


def dot_rows(left, right):
    return lax.dot_general(
        left,
        right,
        (((0,), (0,)), ((), ())),
        precision=lax.Precision.HIGHEST,
        preferred_element_type=F32,
    )


def split(value):
    high = value.astype(jnp.bfloat16)
    return high, (value - high.astype(F32)).astype(jnp.bfloat16)


def dot_split(left, right, dim=1):
    def once(a, b):
        return lax.dot_general(a, b, (((dim,), (0,)), ((), ())), preferred_element_type=F32)

    return once(left[0], right[1]) + once(left[1], right[0]) + once(left[0], right[0])


def exchange(parts, width):
    parts = list(parts)
    count = len(parts)
    segment = lax.broadcasted_iota(jnp.int32, parts[0].shape, 1) // width
    bit = count // 2
    while bit:
        low = (segment % (2 * bit)) < bit
        for a in range(count):
            if a & bit == 0:
                first, second = parts[a], parts[a + bit]
                parts[a] = jnp.where(low, first, pltpu.roll(second, bit * width, 1))
                parts[a + bit] = jnp.where(low, pltpu.roll(first, LANES - bit * width, 1), second)
        bit //= 2
    return parts


def kernel(
    rows,
    cols,
    a_hbm,
    pattern_ref,
    listed_ref,
    panel_hbm,
    link_hbm,
    diag_hbm,
    upper_ref,
    out_ref,
    a_ref,
    panel_ref,
    link_ref,
    diag_ref,
    panels,
    anc,
    slab,
    partial,
    shares,
    left_out,
    left_in,
    kept_out,
    kept_in,
    gather_out,
    gather_in,
    tile_out,
    tile_in,
    extra_out,
    extra_in,
    turned,
    load_sems,
    anc_send,
    anc_recv,
    far_send,
    far_recv,
    gather_got,
    ready,
    sems,
):
    row, col = lax.axis_index("row"), lax.axis_index("col")
    depth = cols // 2
    z, side = lax.div(col, 2), lax.rem(col, 2)
    pair, core = lax.div(row, 2), lax.rem(row, 2)
    pairs = rows // 2
    height = panel_ref.shape[1]
    width = panel_ref.shape[2]
    half = width // 2
    plane = 2 * rows
    me = side * rows + row
    slot_me = (core * 2 + side) * pairs + pair
    tall = a_ref.shape[0]
    band_rows = width // rows
    band_cols = width // cols
    count = cols // 2
    own = lax.div(col, count) == side

    (slab_sent, slab_got, left_sent, left_got, kept_sent, kept_got, share_sent, share_got) = (
        sems.at[i] for i in range(8)
    )
    gather_sent, pass_sent, pass_got, tile_sent, tile_got = (sems.at[i] for i in range(8, 13))
    extra_sent, extra_got, forward_sent, forward_got = (sems.at[i] for i in range(13, 17))

    def wait_for(ref, sem):
        pltpu.make_async_copy(ref, ref, sem).wait()

    def wrap(value, size):
        return jnp.where(value >= size, value - size, value)

    def plane_at(offset):
        return wrap(z + offset % depth, depth)

    def each_peer(act):
        act(row, 1 - side)

        @pl.loop(1, rows)
        def _(step):
            other = wrap(row + step, rows)
            act(other, side)
            act(other, 1 - side)

    def each_chip(act):
        act(pair, 1 - side, 1)

        @pl.loop(1, pairs)
        def _(step):
            other = wrap(pair + step, pairs)
            act(other, side, 2 * step)
            act(other, 1 - side, 2 * step + 1)

    held = [(0, (*HOPS[1:], 0)), (-STRIDE, (*HOPS, 0)), (STRIDE, (*HOPS[1:], 0))]
    own_slab = functools.reduce(jnp.logical_or, [lax.div(plane_at(offset), 2) == pair for offset, _ in held])

    loads = [
        pltpu.make_async_copy(panel_hbm, panel_ref, load_sems.at[0]),
        pltpu.make_async_copy(a_hbm, a_ref, load_sems.at[1]),
        pltpu.make_async_copy(diag_hbm, diag_ref, load_sems.at[2]),
        pltpu.make_async_copy(link_hbm, link_ref, load_sems.at[3]),
    ]
    with jax.named_scope("greet"):
        for load in loads:
            load.start()
        barrier = pltpu.get_barrier_semaphore()

        def greet(device):
            pl.semaphore_signal(barrier, inc=1, device_id=device, device_id_type=MESH)

        for offset in (*HOPS, STRIDE, -STRIDE):
            greet((row, 2 * plane_at(offset) + side))
        each_peer(lambda r, s: greet((r, 2 * z + s)))

        def keep(s):
            found = listed_ref[s, 0] == col
            for i in range(1, listed_ref.shape[1]):
                found = jnp.logical_or(found, listed_ref[s, i] == col)
            return jnp.where(found, 1.0, 0.0).astype(F32)

        flag0, flag1 = keep(0), keep(1)
        loads[0].wait()
        kept0 = panel_ref[0] * flag0
        kept1 = panel_ref[1] * flag1
        panels[0, 0] = kept0
        panels[0, 1] = kept1
        loads[1].wait()
        for i in range(tall // BLK):
            present = pattern_ref[(tall // BLK) * row + i, col].astype(F32)
            anc[side, pl.ds(core * tall + i * BLK, BLK), :] = a_ref[pl.ds(i * BLK, BLK), :] * present
        pl.semaphore_wait(barrier, plane - 1 + len(HOPS) + 2)

    def far_copy(j, super_of):
        return pltpu.make_async_remote_copy(
            src_ref=panels.at[0, super_of],
            dst_ref=panels.at[j, super_of],
            send_sem=far_send.at[j - 1, super_of],
            recv_sem=far_recv.at[j - 1, super_of],
            device_id=(row, 2 * plane_at(STRIDE if j == 1 else -STRIDE) + side),
            device_id_type=MESH,
        )

    def spread(j, super_of):
        back, offsets = held[j]
        block = plane_at(back)
        owner = lax.div(block, 2)
        slot = (lax.rem(block, 2) * 2 + side) * rows + row
        for offset in offsets:
            for step in range(2):
                half_of = side if step == 0 else 1 - side
                source = panels.at[j, super_of, :, pl.ds(pl.multiple_of(half_of * half, LANES), half)]

                def send():
                    pltpu.make_async_remote_copy(
                        src_ref=source,
                        dst_ref=slab.at[slot],
                        send_sem=slab_sent,
                        recv_sem=slab_got,
                        device_id=(2 * owner + super_of, 2 * plane_at(offset) + half_of),
                        device_id_type=MESH,
                    ).start()

                if step == 0 and offset == 0:
                    here = jnp.logical_and(owner == pair, core == super_of)
                    pl.when(jnp.logical_not(here))(send)

                    @pl.when(here)
                    def _():
                        pltpu.make_async_copy(source, slab.at[slot], slab_got).start()
                else:
                    send()

    def anc_copy(i):
        piece = anc.at[1 - side if i == 3 else side, pl.ds(core * tall, tall), :]
        return pltpu.make_async_remote_copy(
            src_ref=piece,
            dst_ref=piece,
            send_sem=anc_send.at[i - 1],
            recv_sem=anc_recv.at[i - 1],
            device_id=(row, 2 * z + 1 - side) if i == 2 else (2 * pair + 1 - core, col),
            device_id_type=MESH,
        )

    def chip_copy(source, target, sent, got):
        return pltpu.make_async_remote_copy(
            src_ref=source,
            dst_ref=target,
            send_sem=sent,
            recv_sem=got,
            device_id=(2 * pair + 1 - core, col),
            device_id_type=MESH,
        )

    with jax.named_scope("start"):
        for super_of in range(2):
            for j in (1, 2):
                far_copy(j, super_of).start()
        for offset in HOPS:
            pl.semaphore_signal(
                ready, inc=1, device_id=(row, 2 * plane_at(-offset) + side), device_id_type=MESH
            )
        for i in (2, 1):
            anc_copy(i).start()

    with jax.named_scope("early"):
        for h in range(2):
            kept_out[h] = kept1[:, h * half : (h + 1) * half]
        kept_in[slot_me] = kept_out[side]

        def send_kept(p, s, _):
            pltpu.make_async_remote_copy(
                src_ref=kept_out.at[s],
                dst_ref=kept_in.at[slot_me],
                send_sem=kept_sent,
                recv_sem=kept_got,
                device_id=(2 * p + core, 2 * z + s),
                device_id_type=MESH,
            ).start()

        loads[2].wait()
        loads[3].wait()
        mixed = kept1 - dot(kept0, link_ref[...])
        link_band = link_ref[pl.ds(pl.multiple_of(row * band_rows, 8), band_rows), :]
        extra = dot(diag_ref[0], link_band)
        for h in range(2):
            extra_out[h] = extra[h * height : (h + 1) * height]
        extra_swap = chip_copy(extra_out.at[1 - core], extra_in, extra_sent, extra_got)
        extra_swap.start()
        pl.semaphore_wait(ready, len(HOPS))
        for super_of in range(2):
            spread(0, super_of)
        each_chip(send_kept)
        extra_swap.wait_recv()
        extra = extra_out[core] + extra_in[...]
        per = LANES // band_rows
        for g in range(width // LANES):
            cut = slice(g * LANES, (g + 1) * LANES)
            packed = exchange([kept0[:, cut], kept1[:, cut], mixed[:, cut], extra[:, cut]], band_rows)
            for j in range(per):
                left_out[g * per + j] = packed[j]
        left_in[slot_me] = left_out[row]

        @each_peer
        def _(r, s):
            pltpu.make_async_remote_copy(
                src_ref=left_out.at[r],
                dst_ref=left_in.at[slot_me],
                send_sem=left_sent,
                recv_sem=left_got,
                device_id=(r, 2 * z + s),
                device_id_type=MESH,
            ).start()

    with jax.named_scope("spread"):
        for super_of in range(2):
            for j in (1, 2):
                far_copy(j, super_of).wait_recv()
                spread(j, super_of)
        anc_copy(2).wait_recv()
        anc_copy(3).start()

    with jax.named_scope("slab"):
        for i in (1, 3):
            anc_copy(i).wait_recv()
        for i in range(2):
            turned[2 * i], turned[2 * i + 1] = split(anc[i].T)
        wait_for(slab, slab_got)
    with jax.named_scope("product"):
        kept_rows = split(slab[...].reshape(2 * tall, half))
        for i in range(2):
            part = dot_split((turned[2 * i], turned[2 * i + 1]), kept_rows)
            partial[pl.ds(i * rows, rows)] = part.reshape(rows, height, half)

    slot = (2 * core + side) * pairs + pair
    with jax.named_scope("scatter"):
        shares[slot] = partial[me]

        @each_peer
        def _(r, s):
            pltpu.make_async_remote_copy(
                src_ref=partial.at[s * rows + r],
                dst_ref=shares.at[slot],
                send_sem=share_sent,
                recv_sem=share_got,
                device_id=(r, 2 * z + s),
                device_id_type=MESH,
            ).start()

    with jax.named_scope("linkterm"):
        wait_for(kept_in.at[pl.ds(0, rows - 1)], kept_got)
        mine = pl.ds(core * rows, rows)
        kept_swap = chip_copy(kept_in.at[mine], kept_in.at[mine], forward_sent, forward_got)
        kept_swap.start()
        wait_for(left_in.at[pl.ds(0, plane - 1)], left_got)
        lefts = left_in[...].reshape(plane * height, LANES)
        column_half = pl.ds(pl.multiple_of(side * half, LANES), half)
        group = pl.ds(pl.multiple_of(lax.div(row, per) * LANES, LANES), LANES)
        link_half = split(link_ref[:, column_half])
        link_group = split(link_ref[:, group])
        link_rows = link_ref[pl.ds(pl.multiple_of(z * 2 * band_cols, 8), 2 * band_cols), column_half]
        repeated = jnp.concatenate(
            [
                link_rows[s * band_cols + k * height : s * band_cols + (k + 1) * height]
                for k in range(2)
                for s in range(2)
                for _ in range(pairs)
            ],
            axis=0,
        )
        constant = pltpu.roll(dot_rows(repeated, lefts), 2 * band_rows, 1)
        first = split(lefts)
        kept_swap.wait_recv()
        kept_half = split(kept_in[...].reshape(plane * height, half))

    with jax.named_scope("shares"):
        wait_for(shares.at[pl.ds(0, plane - 1)], share_got)
        quarters = []
        for q in range(4):
            total = shares[q * pairs]
            for i in range(1, pairs):
                total = total + shares[q * pairs + i]
            quarters.append(total)
        sum0 = jnp.concatenate(quarters[:2], axis=1)
        sum1 = jnp.concatenate(quarters[2:], axis=1)
        upper0 = -sum0 * flag0
        for h in range(2):
            gather_out[h, :, :width] = upper0
            gather_out[h, :, width:] = quarters[2 + h]
        gather_in[slot_me] = gather_out[side]

    with jax.named_scope("gather"):

        @each_chip
        def _(p, s, number):
            pltpu.make_async_remote_copy(
                src_ref=gather_out.at[s],
                dst_ref=gather_in.at[slot_me],
                send_sem=gather_sent,
                recv_sem=gather_got.at[number],
                device_id=(2 * p + core, 2 * z + s),
                device_id_type=MESH,
            ).start()

        chip_copy(gather_in.at[slot_me], gather_in.at[slot_me], pass_sent, pass_got).start()

        def forward(p, s, number):
            arrived = gather_in.at[(core * 2 + s) * pairs + p]
            wait_for(arrived, gather_got.at[number])
            chip_copy(arrived, arrived, pass_sent, pass_got).start()

        forward(pair, 1 - side, 1)

        @pl.loop(1, pairs)
        def _(step):
            other = wrap(pair + pairs - step, pairs)
            forward(other, side, 2 * step)
            forward(other, 1 - side, 2 * step + 1)

        wait_for(gather_in.at[mine], pass_got)

    with jax.named_scope("diagonal"):
        uppers = split(gather_in[:, :, :width].reshape(plane * height, width))
        sums = split(gather_in[:, :, width:].reshape(plane * height, half))
        chained_half = split(dot_split(uppers, link_half))
        chained_group = split(dot_split(uppers, link_group))
        upper_half = split(gather_in[:, :, column_half].reshape(plane * height, half))
        turn = lax.rem(LANES + band_rows - lax.rem(row, per) * band_rows, LANES)
        later = (
            dot_split(sums, first, 0)
            + pltpu.roll(dot_split(chained_half, first, 0), LANES - band_rows, 1)
            + pltpu.roll(dot_split(kept_half, chained_group, 0), turn, 1)
            + constant
        )
        lane = lax.broadcasted_iota(jnp.int32, (half, LANES), 1)
        tiles = jnp.where(lane < band_rows, -dot_split(upper_half, first, 0), later)
        low = lane[:8] < 2 * band_rows
        for j in range(count):
            top = tiles[band_cols * j : band_cols * j + 8]
            bottom = tiles[band_cols * j + 8 : band_cols * j + 16]
            tile_out[j] = jnp.where(low, top, pltpu.roll(bottom, 2 * band_rows, 1))

    def finish_upper():
        upper_ref[0] = upper0
        upper_ref[1] = -(sum1 + dot(upper0, link_ref[...])) * flag1

    with jax.named_scope("tiles"):
        pl.when(side == 1)(finish_upper)

        for other in range(count):
            target = side * count + other

            def send():
                pltpu.make_async_remote_copy(
                    src_ref=tile_out.at[other],
                    dst_ref=tile_in.at[z],
                    send_sem=tile_sent,
                    recv_sem=tile_got,
                    device_id=(row, target),
                    device_id_type=MESH,
                ).start()

            pl.when(target != col)(send)

            @pl.when(target == col)
            def _():
                pltpu.make_async_copy(tile_out.at[other], tile_in.at[z], tile_got).start()

        pl.when(side == 0)(finish_upper)
        wait_for(tile_in, tile_got)
        total = tile_in[0]
        for i in range(1, depth):
            total = total + tile_in[i]
        for i in range(2):
            for s in range(2):
                at = (2 * i + s) * band_rows
                out_ref[s, 8 * i : 8 * i + 8, :] = diag_ref[s, 8 * i : 8 * i + 8, :] + total[:, at : at + band_rows]

    with jax.named_scope("drain"):
        for i in (1, 2, 3):
            anc_copy(i).wait_send()
        for super_of in range(2):
            for j in (1, 2):
                far_copy(j, super_of).wait_send()
        extra_swap.wait_send()
        kept_swap.wait_send()

        @pl.when(own_slab)
        def _():
            wait_for(slab.at[pl.ds(0, 4 * rows - 1)], slab_sent)

        @pl.when(jnp.logical_not(own_slab))
        def _():
            wait_for(slab, slab_sent)

        wait_for(left_in.at[pl.ds(0, plane - 1)], left_sent)
        wait_for(kept_in.at[pl.ds(0, rows - 1)], kept_sent)
        wait_for(shares.at[pl.ds(0, plane - 1)], share_sent)
        wait_for(gather_in.at[pl.ds(0, rows - 1)], gather_sent)
        wait_for(gather_in.at[mine], pass_sent)

        @pl.when(own)
        def _():
            wait_for(tile_in.at[pl.ds(0, count - 1)], tile_sent)

        @pl.when(jnp.logical_not(own))
        def _():
            wait_for(tile_in, tile_sent)


def local(rows, cols, ancestor_inverse, pattern, listed, panels, parent_panels, diag_inverse):
    supers, height, width = panels.shape
    tall, wide = ancestor_inverse.shape
    depth = cols // 2
    plane = 2 * rows
    half = width // 2
    count = cols // 2
    vmem = pl.BlockSpec(memory_space=pltpu.VMEM)
    smem = pl.BlockSpec(memory_space=pltpu.SMEM)
    anywhere = pl.BlockSpec(memory_space=pl.ANY)
    turned = jnp.swapaxes(diag_inverse, 1, 2)
    upper, tiles = pl.pallas_call(
        functools.partial(kernel, rows, cols),
        out_shape=(
            jax.ShapeDtypeStruct(panels.shape, F32),
            jax.ShapeDtypeStruct(turned.shape, F32),
        ),
        in_specs=[anywhere, smem, smem, anywhere, anywhere, anywhere],
        out_specs=(vmem, vmem),
        scratch_shapes=[
            pltpu.VMEM(ancestor_inverse.shape, F32),
            pltpu.VMEM(panels.shape, F32),
            pltpu.VMEM((width, width), F32),
            pltpu.VMEM(turned.shape, F32),
            pltpu.VMEM((3, supers, height, width), F32),
            pltpu.VMEM((2, 2 * tall, wide), F32),
            pltpu.VMEM((4 * rows, height, half), F32),
            pltpu.VMEM((plane, height, half), F32),
            pltpu.VMEM((plane, height, half), F32),
            pltpu.VMEM((rows, height, LANES), F32),
            pltpu.VMEM((plane, height, LANES), F32),
            pltpu.VMEM((2, height, half), F32),
            pltpu.VMEM((plane, height, half), F32),
            pltpu.VMEM((2, height, width + half), F32),
            pltpu.VMEM((plane, height, width + half), F32),
            pltpu.VMEM((count, 8, LANES), F32),
            pltpu.VMEM((depth, 8, LANES), F32),
            pltpu.VMEM((2, height, width), F32),
            pltpu.VMEM((height, width), F32),
            pltpu.VMEM((4, wide, 2 * tall), jnp.bfloat16),
            pltpu.SemaphoreType.DMA((4,)),
            pltpu.SemaphoreType.DMA((3,)),
            pltpu.SemaphoreType.DMA((3,)),
            pltpu.SemaphoreType.DMA((2, 2)),
            pltpu.SemaphoreType.DMA((2, 2)),
            pltpu.SemaphoreType.DMA((rows,)),
            pltpu.SemaphoreType.REGULAR,
            pltpu.SemaphoreType.DMA((17,)),
        ],
        compiler_params=pltpu.CompilerParams(
            collective_id=0, has_side_effects=True, vmem_limit_bytes=56 * 1024 * 1024
        ),
    )(ancestor_inverse, pattern, listed, panels, parent_panels[0], turned)
    return upper, jnp.swapaxes(tiles, 1, 2)


def solution(mesh):
    rows, cols = mesh.shape["row"], mesh.shape["col"]
    return jax.shard_map(
        functools.partial(local, rows, cols),
        mesh=mesh,
        in_specs=(
            P("row", "col"),
            P(),
            P(),
            P(None, ("col", "row"), None),
            P(),
            P(None, "row", "col"),
        ),
        out_specs=(P(None, ("col", "row"), None), P(None, "row", "col")),
        check_vma=False,
    )
```

```python
import functools

import jax
import jax.numpy as jnp
from jax import lax
from jax.experimental import pallas as pl
from jax.experimental.pallas import tpu as pltpu
from jax.sharding import PartitionSpec as P

BLK = 128
LANES = 128
STRIDE = 5
HOPS = (3, 2, -2, 1, -1)
MESH = pl.DeviceIdType.MESH
F32 = jnp.float32


def dot(left, right):
    return jnp.dot(left, right, precision=lax.Precision.HIGHEST, preferred_element_type=F32)


def dot_rows(left, right):
    return lax.dot_general(
        left,
        right,
        (((0,), (0,)), ((), ())),
        precision=lax.Precision.HIGHEST,
        preferred_element_type=F32,
    )


def split(value):
    high = value.astype(jnp.bfloat16)
    return high, (value - high.astype(F32)).astype(jnp.bfloat16)


def dot_split(left, right, dim=1):
    def once(a, b):
        return lax.dot_general(a, b, (((dim,), (0,)), ((), ())), preferred_element_type=F32)

    return once(left[0], right[1]) + once(left[1], right[0]) + once(left[0], right[0])


def exchange(parts, width):
    parts = list(parts)
    count = len(parts)
    segment = lax.broadcasted_iota(jnp.int32, parts[0].shape, 1) // width
    bit = count // 2
    while bit:
        low = (segment % (2 * bit)) < bit
        for a in range(count):
            if a & bit == 0:
                first, second = parts[a], parts[a + bit]
                parts[a] = jnp.where(low, first, pltpu.roll(second, bit * width, 1))
                parts[a + bit] = jnp.where(low, pltpu.roll(first, LANES - bit * width, 1), second)
        bit //= 2
    return parts


def kernel(
    rows,
    cols,
    a_hbm,
    pattern_ref,
    listed_ref,
    panel_hbm,
    link_hbm,
    diag_hbm,
    upper_ref,
    out_ref,
    a_ref,
    panel_ref,
    link_ref,
    diag_ref,
    panels,
    anc,
    slab,
    partial,
    shares,
    left_out,
    left_in,
    kept_out,
    kept_in,
    gather_out,
    gather_in,
    tile_out,
    tile_in,
    extra_out,
    extra_in,
    turned,
    load_sems,
    anc_send,
    anc_recv,
    far_send,
    far_recv,
    gather_got,
    ready,
    sems,
):
    row, col = lax.axis_index("row"), lax.axis_index("col")
    depth = cols // 2
    z, side = lax.div(col, 2), lax.rem(col, 2)
    pair, core = lax.div(row, 2), lax.rem(row, 2)
    pairs = rows // 2
    height = panel_ref.shape[1]
    width = panel_ref.shape[2]
    half = width // 2
    plane = 2 * rows
    me = side * rows + row
    slot_me = (core * 2 + side) * pairs + pair
    tall = a_ref.shape[0]
    band_rows = width // rows
    band_cols = width // cols
    count = cols // 2
    own = lax.div(col, count) == side

    (slab_sent, slab_got, left_sent, left_got, kept_sent, kept_got, share_sent, share_got) = (
        sems.at[i] for i in range(8)
    )
    gather_sent, pass_sent, pass_got, tile_sent, tile_got = (sems.at[i] for i in range(8, 13))
    extra_sent, extra_got, forward_sent, forward_got = (sems.at[i] for i in range(13, 17))

    def wait_for(ref, sem):
        pltpu.make_async_copy(ref, ref, sem).wait()

    def wrap(value, size):
        return jnp.where(value >= size, value - size, value)

    def plane_at(offset):
        return wrap(z + offset % depth, depth)

    def each_peer(act):
        act(row, 1 - side)

        @pl.loop(1, rows)
        def _(step):
            other = wrap(row + step, rows)
            act(other, side)
            act(other, 1 - side)

    def each_chip(act):
        act(pair, 1 - side, 1)

        @pl.loop(1, pairs)
        def _(step):
            other = wrap(pair + step, pairs)
            act(other, side, 2 * step)
            act(other, 1 - side, 2 * step + 1)

    held = [(0, (*HOPS[1:], 0)), (-STRIDE, (*HOPS, 0)), (STRIDE, (*HOPS[1:], 0))]
    own_slab = functools.reduce(jnp.logical_or, [lax.div(plane_at(offset), 2) == pair for offset, _ in held])

    loads = [
        pltpu.make_async_copy(panel_hbm, panel_ref, load_sems.at[0]),
        pltpu.make_async_copy(a_hbm, a_ref, load_sems.at[1]),
        pltpu.make_async_copy(diag_hbm, diag_ref, load_sems.at[2]),
        pltpu.make_async_copy(link_hbm, link_ref, load_sems.at[3]),
    ]
    with jax.named_scope("greet"):
        for load in loads:
            load.start()
        barrier = pltpu.get_barrier_semaphore()

        def greet(device):
            pl.semaphore_signal(barrier, inc=1, device_id=device, device_id_type=MESH)

        for offset in (*HOPS, STRIDE, -STRIDE):
            greet((row, 2 * plane_at(offset) + side))
        each_peer(lambda r, s: greet((r, 2 * z + s)))

        def keep(s):
            found = listed_ref[s, 0] == col
            for i in range(1, listed_ref.shape[1]):
                found = jnp.logical_or(found, listed_ref[s, i] == col)
            return jnp.where(found, 1.0, 0.0).astype(F32)

        flag0, flag1 = keep(0), keep(1)
        loads[0].wait()
        kept0 = panel_ref[0] * flag0
        kept1 = panel_ref[1] * flag1
        panels[0, 0] = kept0
        panels[0, 1] = kept1
        loads[1].wait()
        for i in range(tall // BLK):
            present = pattern_ref[(tall // BLK) * row + i, col].astype(F32)
            anc[side, pl.ds(core * tall + i * BLK, BLK), :] = a_ref[pl.ds(i * BLK, BLK), :] * present
        pl.semaphore_wait(barrier, plane - 1 + len(HOPS) + 2)

    def far_copy(j, super_of):
        return pltpu.make_async_remote_copy(
            src_ref=panels.at[0, super_of],
            dst_ref=panels.at[j, super_of],
            send_sem=far_send.at[j - 1, super_of],
            recv_sem=far_recv.at[j - 1, super_of],
            device_id=(row, 2 * plane_at(STRIDE if j == 1 else -STRIDE) + side),
            device_id_type=MESH,
        )

    def spread(j, super_of):
        back, offsets = held[j]
        block = plane_at(back)
        owner = lax.div(block, 2)
        slot = (lax.rem(block, 2) * 2 + side) * rows + row
        for offset in offsets:
            for step in range(2):
                half_of = side if step == 0 else 1 - side
                source = panels.at[j, super_of, :, pl.ds(pl.multiple_of(half_of * half, LANES), half)]

                def send():
                    pltpu.make_async_remote_copy(
                        src_ref=source,
                        dst_ref=slab.at[slot],
                        send_sem=slab_sent,
                        recv_sem=slab_got,
                        device_id=(2 * owner + super_of, 2 * plane_at(offset) + half_of),
                        device_id_type=MESH,
                    ).start()

                if step == 0 and offset == 0:
                    here = jnp.logical_and(owner == pair, core == super_of)
                    pl.when(jnp.logical_not(here))(send)

                    @pl.when(here)
                    def _():
                        pltpu.make_async_copy(source, slab.at[slot], slab_got).start()
                else:
                    send()

    def anc_copy(i):
        piece = anc.at[1 - side if i == 3 else side, pl.ds(core * tall, tall), :]
        return pltpu.make_async_remote_copy(
            src_ref=piece,
            dst_ref=piece,
            send_sem=anc_send.at[i - 1],
            recv_sem=anc_recv.at[i - 1],
            device_id=(row, 2 * z + 1 - side) if i == 2 else (2 * pair + 1 - core, col),
            device_id_type=MESH,
        )

    def chip_copy(source, target, sent, got):
        return pltpu.make_async_remote_copy(
            src_ref=source,
            dst_ref=target,
            send_sem=sent,
            recv_sem=got,
            device_id=(2 * pair + 1 - core, col),
            device_id_type=MESH,
        )

    with jax.named_scope("start"):
        for super_of in range(2):
            for j in (1, 2):
                far_copy(j, super_of).start()
        for offset in HOPS:
            pl.semaphore_signal(
                ready, inc=1, device_id=(row, 2 * plane_at(-offset) + side), device_id_type=MESH
            )
        anc_copy(2).start()

    with jax.named_scope("early"):
        for h in range(2):
            kept_out[h] = kept1[:, h * half : (h + 1) * half]
        kept_in[slot_me] = kept_out[side]

        def send_kept(p, s, _):
            pltpu.make_async_remote_copy(
                src_ref=kept_out.at[s],
                dst_ref=kept_in.at[slot_me],
                send_sem=kept_sent,
                recv_sem=kept_got,
                device_id=(2 * p + core, 2 * z + s),
                device_id_type=MESH,
            ).start()

        loads[2].wait()
        loads[3].wait()
        mixed = kept1 - dot(kept0, link_ref[...])
        link_band = link_ref[pl.ds(pl.multiple_of(row * band_rows, 8), band_rows), :]
        extra = dot(diag_ref[0], link_band)
        for h in range(2):
            extra_out[h] = extra[h * height : (h + 1) * height]
        extra_swap = chip_copy(extra_out.at[1 - core], extra_in, extra_sent, extra_got)
        extra_swap.start()
        anc_copy(1).start()
        pl.semaphore_wait(ready, len(HOPS))
        for super_of in range(2):
            spread(0, super_of)
        each_chip(send_kept)
        extra_swap.wait_recv()
        extra = extra_out[core] + extra_in[...]
        per = LANES // band_rows
        for g in range(width // LANES):
            cut = slice(g * LANES, (g + 1) * LANES)
            packed = exchange([kept0[:, cut], kept1[:, cut], mixed[:, cut], extra[:, cut]], band_rows)
            for j in range(per):
                left_out[g * per + j] = packed[j]
        left_in[slot_me] = left_out[row]

        @each_peer
        def _(r, s):
            pltpu.make_async_remote_copy(
                src_ref=left_out.at[r],
                dst_ref=left_in.at[slot_me],
                send_sem=left_sent,
                recv_sem=left_got,
                device_id=(r, 2 * z + s),
                device_id_type=MESH,
            ).start()

    with jax.named_scope("spread"):
        for super_of in range(2):
            for j in (1, 2):
                far_copy(j, super_of).wait_recv()
                spread(j, super_of)
        anc_copy(2).wait_recv()
        anc_copy(3).start()

    with jax.named_scope("slab"):
        for i in (1, 3):
            anc_copy(i).wait_recv()
        for i in range(2):
            turned[2 * i], turned[2 * i + 1] = split(anc[i].T)
        wait_for(slab, slab_got)
    with jax.named_scope("product"):
        kept_rows = split(slab[...].reshape(2 * tall, half))
        for i in range(2):
            part = dot_split((turned[2 * i], turned[2 * i + 1]), kept_rows)
            partial[pl.ds(i * rows, rows)] = part.reshape(rows, height, half)

    slot = (2 * core + side) * pairs + pair
    with jax.named_scope("scatter"):
        shares[slot] = partial[me]

        @each_peer
        def _(r, s):
            pltpu.make_async_remote_copy(
                src_ref=partial.at[s * rows + r],
                dst_ref=shares.at[slot],
                send_sem=share_sent,
                recv_sem=share_got,
                device_id=(r, 2 * z + s),
                device_id_type=MESH,
            ).start()

    with jax.named_scope("linkterm"):
        wait_for(kept_in.at[pl.ds(0, rows - 1)], kept_got)
        mine = pl.ds(core * rows, rows)
        kept_swap = chip_copy(kept_in.at[mine], kept_in.at[mine], forward_sent, forward_got)
        kept_swap.start()
        wait_for(left_in.at[pl.ds(0, plane - 1)], left_got)
        lefts = left_in[...].reshape(plane * height, LANES)
        column_half = pl.ds(pl.multiple_of(side * half, LANES), half)
        group = pl.ds(pl.multiple_of(lax.div(row, per) * LANES, LANES), LANES)
        link_half = split(link_ref[:, column_half])
        link_group = split(link_ref[:, group])
        link_rows = link_ref[pl.ds(pl.multiple_of(z * 2 * band_cols, 8), 2 * band_cols), column_half]
        repeated = jnp.concatenate(
            [
                link_rows[s * band_cols + k * height : s * band_cols + (k + 1) * height]
                for k in range(2)
                for s in range(2)
                for _ in range(pairs)
            ],
            axis=0,
        )
        constant = pltpu.roll(dot_rows(repeated, lefts), 2 * band_rows, 1)
        first = split(lefts)
        kept_swap.wait_recv()
        kept_half = split(kept_in[...].reshape(plane * height, half))

    with jax.named_scope("shares"):
        wait_for(shares.at[pl.ds(0, plane - 1)], share_got)
        quarters = []
        for q in range(4):
            total = shares[q * pairs]
            for i in range(1, pairs):
                total = total + shares[q * pairs + i]
            quarters.append(total)
        sum0 = jnp.concatenate(quarters[:2], axis=1)
        sum1 = jnp.concatenate(quarters[2:], axis=1)
        upper0 = -sum0 * flag0
        for h in range(2):
            gather_out[h, :, :width] = upper0
            gather_out[h, :, width:] = quarters[2 + h]
        gather_in[slot_me] = gather_out[side]

    with jax.named_scope("gather"):

        @each_chip
        def _(p, s, number):
            pltpu.make_async_remote_copy(
                src_ref=gather_out.at[s],
                dst_ref=gather_in.at[slot_me],
                send_sem=gather_sent,
                recv_sem=gather_got.at[number],
                device_id=(2 * p + core, 2 * z + s),
                device_id_type=MESH,
            ).start()

        chip_copy(gather_in.at[slot_me], gather_in.at[slot_me], pass_sent, pass_got).start()

        def forward(p, s, number):
            arrived = gather_in.at[(core * 2 + s) * pairs + p]
            wait_for(arrived, gather_got.at[number])
            chip_copy(arrived, arrived, pass_sent, pass_got).start()

        forward(pair, 1 - side, 1)

        @pl.loop(1, pairs)
        def _(step):
            other = wrap(pair + pairs - step, pairs)
            forward(other, side, 2 * step)
            forward(other, 1 - side, 2 * step + 1)

        wait_for(gather_in.at[mine], pass_got)

    with jax.named_scope("diagonal"):
        uppers = split(gather_in[:, :, :width].reshape(plane * height, width))
        sums = split(gather_in[:, :, width:].reshape(plane * height, half))
        chained_half = split(dot_split(uppers, link_half))
        chained_group = split(dot_split(uppers, link_group))
        upper_half = split(gather_in[:, :, column_half].reshape(plane * height, half))
        turn = lax.rem(LANES + band_rows - lax.rem(row, per) * band_rows, LANES)
        later = (
            dot_split(sums, first, 0)
            + pltpu.roll(dot_split(chained_half, first, 0), LANES - band_rows, 1)
            + pltpu.roll(dot_split(kept_half, chained_group, 0), turn, 1)
            + constant
        )
        lane = lax.broadcasted_iota(jnp.int32, (half, LANES), 1)
        tiles = jnp.where(lane < band_rows, -dot_split(upper_half, first, 0), later)
        low = lane[:8] < 2 * band_rows
        for j in range(count):
            top = tiles[band_cols * j : band_cols * j + 8]
            bottom = tiles[band_cols * j + 8 : band_cols * j + 16]
            tile_out[j] = jnp.where(low, top, pltpu.roll(bottom, 2 * band_rows, 1))

    def finish_upper():
        upper_ref[0] = upper0
        upper_ref[1] = -(sum1 + dot(upper0, link_ref[...])) * flag1

    with jax.named_scope("tiles"):
        pl.when(side == 1)(finish_upper)

        for other in (2, 3, 4, 5, 6, 7, 0, 1, *range(8, count)):
            target = side * count + other

            def send():
                pltpu.make_async_remote_copy(
                    src_ref=tile_out.at[other],
                    dst_ref=tile_in.at[z],
                    send_sem=tile_sent,
                    recv_sem=tile_got,
                    device_id=(row, target),
                    device_id_type=MESH,
                ).start()

            pl.when(target != col)(send)

            @pl.when(target == col)
            def _():
                pltpu.make_async_copy(tile_out.at[other], tile_in.at[z], tile_got).start()

        pl.when(side == 0)(finish_upper)
        wait_for(tile_in, tile_got)
        total = tile_in[0]
        for i in range(1, depth):
            total = total + tile_in[i]
        for i in range(2):
            for s in range(2):
                at = (2 * i + s) * band_rows
                out_ref[s, 8 * i : 8 * i + 8, :] = diag_ref[s, 8 * i : 8 * i + 8, :] + total[:, at : at + band_rows]

    with jax.named_scope("drain"):
        for i in (1, 2, 3):
            anc_copy(i).wait_send()
        for super_of in range(2):
            for j in (1, 2):
                far_copy(j, super_of).wait_send()
        extra_swap.wait_send()
        kept_swap.wait_send()

        @pl.when(own_slab)
        def _():
            wait_for(slab.at[pl.ds(0, 4 * rows - 1)], slab_sent)

        @pl.when(jnp.logical_not(own_slab))
        def _():
            wait_for(slab, slab_sent)

        wait_for(left_in.at[pl.ds(0, plane - 1)], left_sent)
        wait_for(kept_in.at[pl.ds(0, rows - 1)], kept_sent)
        wait_for(shares.at[pl.ds(0, plane - 1)], share_sent)
        wait_for(gather_in.at[pl.ds(0, rows - 1)], gather_sent)
        wait_for(gather_in.at[mine], pass_sent)

        @pl.when(own)
        def _():
            wait_for(tile_in.at[pl.ds(0, count - 1)], tile_sent)

        @pl.when(jnp.logical_not(own))
        def _():
            wait_for(tile_in, tile_sent)


def local(rows, cols, ancestor_inverse, pattern, listed, panels, parent_panels, diag_inverse):
    supers, height, width = panels.shape
    tall, wide = ancestor_inverse.shape
    depth = cols // 2
    plane = 2 * rows
    half = width // 2
    count = cols // 2
    vmem = pl.BlockSpec(memory_space=pltpu.VMEM)
    smem = pl.BlockSpec(memory_space=pltpu.SMEM)
    anywhere = pl.BlockSpec(memory_space=pl.ANY)
    turned = jnp.swapaxes(diag_inverse, 1, 2)
    upper, tiles = pl.pallas_call(
        functools.partial(kernel, rows, cols),
        out_shape=(
            jax.ShapeDtypeStruct(panels.shape, F32),
            jax.ShapeDtypeStruct(turned.shape, F32),
        ),
        in_specs=[anywhere, smem, smem, anywhere, anywhere, anywhere],
        out_specs=(vmem, vmem),
        scratch_shapes=[
            pltpu.VMEM(ancestor_inverse.shape, F32),
            pltpu.VMEM(panels.shape, F32),
            pltpu.VMEM((width, width), F32),
            pltpu.VMEM(turned.shape, F32),
            pltpu.VMEM((3, supers, height, width), F32),
            pltpu.VMEM((2, 2 * tall, wide), F32),
            pltpu.VMEM((4 * rows, height, half), F32),
            pltpu.VMEM((plane, height, half), F32),
            pltpu.VMEM((plane, height, half), F32),
            pltpu.VMEM((rows, height, LANES), F32),
            pltpu.VMEM((plane, height, LANES), F32),
            pltpu.VMEM((2, height, half), F32),
            pltpu.VMEM((plane, height, half), F32),
            pltpu.VMEM((2, height, width + half), F32),
            pltpu.VMEM((plane, height, width + half), F32),
            pltpu.VMEM((count, 8, LANES), F32),
            pltpu.VMEM((depth, 8, LANES), F32),
            pltpu.VMEM((2, height, width), F32),
            pltpu.VMEM((height, width), F32),
            pltpu.VMEM((4, wide, 2 * tall), jnp.bfloat16),
            pltpu.SemaphoreType.DMA((4,)),
            pltpu.SemaphoreType.DMA((3,)),
            pltpu.SemaphoreType.DMA((3,)),
            pltpu.SemaphoreType.DMA((2, 2)),
            pltpu.SemaphoreType.DMA((2, 2)),
            pltpu.SemaphoreType.DMA((rows,)),
            pltpu.SemaphoreType.REGULAR,
            pltpu.SemaphoreType.DMA((17,)),
        ],
        compiler_params=pltpu.CompilerParams(
            collective_id=0, has_side_effects=True, vmem_limit_bytes=56 * 1024 * 1024
        ),
    )(ancestor_inverse, pattern, listed, panels, parent_panels[0], turned)
    return upper, jnp.swapaxes(tiles, 1, 2)


def solution(mesh):
    rows, cols = mesh.shape["row"], mesh.shape["col"]
    return jax.shard_map(
        functools.partial(local, rows, cols),
        mesh=mesh,
        in_specs=(
            P("row", "col"),
            P(),
            P(),
            P(None, ("col", "row"), None),
            P(),
            P(None, "row", "col"),
        ),
        out_specs=(P(None, ("col", "row"), None), P(None, "row", "col")),
        check_vma=False,
    )
```
